256 devices in a mesh: mem: 32 (over z, x), fsdp: 8 (over y, core).
Axes of the slice: x: 4, y: 4, z: 8, core: 2. Of those that a mesh axis runs over, the one named last changes fastest.
Arguments:
- layer_input: bfloat16 [32768, 4096], P(('mem', 'fsdp')), may hold values from -6 to 6
- w_query: bfloat16 [4096, 2048], P('mem', 'fsdp'), may hold values from -0.09375 to 0.09375
- local_kv: bfloat16 [2, 32768, 2048], P(None, 'mem', 'fsdp'), may hold values from -200 to 200, as said below
- memory_kv: bfloat16 [512, 2, 128, 2048], P('mem', None, None, 'fsdp'), may hold values from -200 to 200
- memory_ids: int32 [256, 4], P('mem'), may hold values from 0 to 511, as said below
- grad_out: bfloat16 [32768, 2048], P('mem', 'fsdp'), may hold values from -6 to 6
Outputs:
- attended: bfloat16 [32768, 2048], P('mem', 'fsdp')
- grad_input: bfloat16 [32768, 4096], P(('mem', 'fsdp'))
The draws below stay inside these ranges and needn't reach their ends.
Inputs may be any that keep to these rules, and one draw needn't show every extreme that they name: `memory_ids`: within the tiles of one local context (8 tiles), all named blocks of one owner (same id // 16) are one and the same block, and every owner is named by some tile of every local context; each tile names 4 blocks of different owners. `local_kv`: keys and values of the document's tokens.
All inputs are finite; a program needn't handle non-finite values.
Results may differ from the reference program's by a relative error of at most 0.025.
The reference program's roundings to bfloat16 on the way count: a program that leaves them out, or rounds other values in their place, can miss the bound.
Values may be sent and summed in bfloat16 or wider, within the bound.
No kernel may reach another device: no remote copies, remote signals or barrier semaphores. Data moves between devices by JAX's collectives and lax.ppermute only.
A program may use at most 128 MiB of HBM per device.

```python
import math
import jax
import jax.numpy as jnp
from jax import lax

D = 4096
HD = 128
BLK = 128
TOPK = 4
MB_DEV = 16
HW = 2048
CTX = 1024
LEN = 32768
TILES = 256
MEMBLK = 512
N_FSDP = 8


def key_rows(key, rows_count, width):
    first_key = jax.random.fold_in(key, 0)
    return jnp.clip(jax.random.normal(first_key, (rows_count, width), jnp.float32), -4.0, 4.0)


def value_rows(key, rows_count, width):
    return jnp.clip(jax.random.normal(key, (rows_count, width), jnp.float32), -4.0, 4.0)


def draw_local_kv(key, part):
    keys_part = key_rows(jax.random.fold_in(key, 11), LEN, HW)
    values_part = value_rows(jax.random.fold_in(key, 12), LEN, HW)
    return jnp.stack([keys_part, values_part]).astype(jnp.bfloat16)


def draw_memory_kv(key, part):
    keys_part = key_rows(jax.random.fold_in(key, 21), MEMBLK * BLK, HW).reshape(MEMBLK, BLK, HW)
    values_part = value_rows(jax.random.fold_in(key, 22), MEMBLK * BLK, HW).reshape(MEMBLK, BLK, HW)
    return jnp.stack([keys_part, values_part], axis=1).astype(jnp.bfloat16)


def draw_memory_ids(key, part):
    owners_count = MEMBLK // MB_DEV
    groups = LEN // CTX
    tiles_per_group = CTX // BLK
    slots_count = tiles_per_group * TOPK
    first_key, second_key, third_key = jax.random.split(jax.random.fold_in(key, 31), 3)
    local_pick = jax.random.randint(first_key, (groups, owners_count), 0, MB_DEV)
    group_keys = jax.random.split(second_key, groups)
    orders = jax.vmap(lambda one_key: jax.random.permutation(one_key, owners_count))(group_keys).astype(jnp.int32)
    rotation = jax.random.randint(third_key, (groups, 1), 0, owners_count)
    slot_index = jnp.arange(slots_count, dtype=jnp.int32)
    positions = (slot_index[None, :] + rotation) % owners_count
    owners = jnp.take_along_axis(orders, positions, axis=1)
    local_part = jnp.take_along_axis(local_pick, owners, axis=1)
    block_ids = owners * MB_DEV + local_part
    return block_ids.reshape(TILES, TOPK).astype(jnp.int32)


def block_scale(own_key, shape, cuts, smallest, top_value):
    level, own = 1.0, jax.random.fold_in(own_key, 6)
    for position, parts in cuts:
        steps = jnp.exp(jax.random.uniform(jax.random.fold_in(own, position), (parts,), jnp.float32, smallest / len(cuts), top_value / len(cuts)))
        level = level * jnp.repeat(steps, shape[position] // parts).reshape([-1 if axis == position else 1 for axis in range(len(shape))])
    return level


def centred(own_key, extent, spread, most, cuts=(), kind=jnp.bfloat16):
    factor_of = block_scale(own_key, extent, cuts, -0.22, 0.18) if cuts else 1.0
    drawn = jax.random.normal(own_key, extent, jnp.float32) * spread * factor_of
    return jnp.minimum(jnp.maximum(drawn, -most), most).astype(kind)


def setup_inputs(seed: int = 0) -> dict:
    key_of = jax.random.split(jax.random.key(seed), 7)
    layer_input = centred(key_of[0], (LEN, D), 1.0, 6.0, ((0, 256),))
    w_query = centred(key_of[1], (D, HW), D ** -0.5, 0.09375, ((0, 32), (1, 8)))
    local_kv = draw_local_kv(jax.random.fold_in(key_of[6], 71), 0)
    memory_kv = draw_memory_kv(jax.random.fold_in(key_of[6], 71), 0)
    memory_ids = draw_memory_ids(jax.random.fold_in(key_of[6], 71), 0)
    grad_out = centred(key_of[5], (LEN, HW), 1.0, 6.0, ((0, 32), (1, 8)))
    return dict(layer_input=layer_input, w_query=w_query, local_kv=local_kv, memory_kv=memory_kv, memory_ids=memory_ids, grad_out=grad_out)


NEG_FILL = -1e+30

def attend_context(queries, context_kv, tile_kv, grad_rows):
    ctx_len, width = queries.shape
    heads_count = width // HD
    tiles_count = tile_kv.shape[0]
    mem_keys_count = TOPK * BLK
    score_scale = 1.0 / math.sqrt(HD)
    query_heads = queries.astype(jnp.float32).reshape(ctx_len, heads_count, HD)
    query_tiles = query_heads.reshape(tiles_count, BLK, heads_count, HD)
    local_keys = context_kv[0].astype(jnp.float32).reshape(ctx_len, heads_count, HD)
    local_values = context_kv[1].astype(jnp.float32).reshape(ctx_len, heads_count, HD)
    mem_keys = tile_kv[:, :, 0].astype(jnp.float32).reshape(tiles_count, mem_keys_count, heads_count, HD)
    mem_values = tile_kv[:, :, 1].astype(jnp.float32).reshape(tiles_count, mem_keys_count, heads_count, HD)
    grad_heads = grad_rows.astype(jnp.float32).reshape(ctx_len, heads_count, HD)
    grad_tiles = grad_heads.reshape(tiles_count, BLK, heads_count, HD)
    mem_scores = jnp.einsum('tqhd,tkhd->htqk', query_tiles, mem_keys) * score_scale
    mem_scores = mem_scores.reshape(heads_count, ctx_len, mem_keys_count)
    loc_scores = jnp.einsum('qhd,khd->hqk', query_heads, local_keys) * score_scale
    positions = jnp.arange(ctx_len, dtype=jnp.int32)
    causal = positions[:, None] >= positions[None, :]
    loc_scores = jnp.where(causal[None], loc_scores, NEG_FILL)
    row_max = jnp.maximum(lax.optimization_barrier(jnp.max(mem_scores, axis=2)), lax.optimization_barrier(jnp.max(loc_scores, axis=2)))
    mem_exp = jnp.exp(mem_scores - row_max[:, :, None])
    loc_exp = jnp.exp(loc_scores - row_max[:, :, None])
    total = lax.optimization_barrier(jnp.sum(mem_exp, axis=2)) + lax.optimization_barrier(jnp.sum(loc_exp, axis=2))
    mem_prob = mem_exp / total[:, :, None]
    loc_prob = loc_exp / total[:, :, None]
    mem_weights = lax.optimization_barrier(mem_prob.astype(jnp.bfloat16)).astype(jnp.float32)
    loc_weights = lax.optimization_barrier(loc_prob.astype(jnp.bfloat16)).astype(jnp.float32)
    mem_part = jnp.einsum('htqk,tkhd->tqhd', mem_weights.reshape(heads_count, tiles_count, BLK, mem_keys_count), mem_values)
    loc_part = jnp.einsum('hqk,khd->qhd', loc_weights, local_values)
    attended = (mem_part.reshape(ctx_len, heads_count, HD) + loc_part).reshape(ctx_len, width).astype(jnp.bfloat16)
    mem_dprob = jnp.einsum('tqhd,tkhd->htqk', grad_tiles, mem_values).reshape(heads_count, ctx_len, mem_keys_count)
    loc_dprob = jnp.einsum('qhd,khd->hqk', grad_heads, local_values)
    delta = lax.optimization_barrier(jnp.sum(mem_prob * mem_dprob, axis=2)) + lax.optimization_barrier(jnp.sum(loc_prob * loc_dprob, axis=2))
    mem_dscore = (mem_prob * (mem_dprob - delta[:, :, None])).astype(jnp.bfloat16)
    loc_dscore = (loc_prob * (loc_dprob - delta[:, :, None])).astype(jnp.bfloat16)
    mem_dscore = lax.optimization_barrier(mem_dscore).astype(jnp.float32)
    loc_dscore = lax.optimization_barrier(loc_dscore).astype(jnp.float32)
    mem_grad = jnp.einsum('htqk,tkhd->tqhd', mem_dscore.reshape(heads_count, tiles_count, BLK, mem_keys_count), mem_keys)
    loc_grad = jnp.einsum('hqk,khd->qhd', loc_dscore, local_keys)
    grad_queries = ((mem_grad.reshape(ctx_len, heads_count, HD) + loc_grad) * score_scale).reshape(ctx_len, width)
    return (attended, grad_queries.astype(jnp.bfloat16))

def reference(layer_input, w_query, local_kv, memory_kv, memory_ids, grad_out):
    queries = jnp.dot(layer_input, w_query, preferred_element_type=jnp.float32).astype(jnp.bfloat16)
    tiles_per_context = CTX // BLK

    def one_context(context_index):
        row_first = (context_index * CTX).astype(jnp.int32)
        tile_first = (context_index * tiles_per_context).astype(jnp.int32)
        query_rows = lax.dynamic_slice_in_dim(queries, row_first, CTX, 0)
        context_kv = lax.dynamic_slice_in_dim(local_kv, row_first, CTX, 1)
        grad_rows = lax.dynamic_slice_in_dim(grad_out, row_first, CTX, 0)
        block_ids = lax.dynamic_slice_in_dim(memory_ids, tile_first, tiles_per_context, 0)
        tile_kv = jnp.take(memory_kv, block_ids, axis=0)
        return attend_context(query_rows, context_kv, tile_kv, grad_rows)
    attended, grad_queries = lax.map(one_context, jnp.arange(LEN // CTX, dtype=jnp.int32))
    attended = attended.reshape(LEN, HW)
    grad_queries = grad_queries.reshape(LEN, HW)
    group_cols = HW // N_FSDP
    grad_total = jnp.zeros((LEN, D), jnp.float32)
    for group in range(N_FSDP):
        grad_cols = grad_queries[:, group * group_cols:(group + 1) * group_cols]
        weight_cols = w_query[:, group * group_cols:(group + 1) * group_cols]
        partial_sum = lax.dot_general(grad_cols, weight_cols, (((1,), (1,)), ((), ())), preferred_element_type=jnp.float32)
        grad_total = grad_total + lax.optimization_barrier(partial_sum.astype(jnp.bfloat16)).astype(jnp.float32)
    return (attended, grad_total.astype(jnp.bfloat16))
```

```python
import functools
import math

import jax
import jax.numpy as jnp
from jax import lax
from jax.experimental import pallas as pl
from jax.experimental.pallas import tpu as pltpu
from jax.sharding import Mesh
from jax.sharding import PartitionSpec as P

HD = 128
BLK = 128
TOPK = 4
MB_DEV = 16
CTX = 1024
TILES = CTX // BLK
ZN, XN, YN, CN = 8, 4, 4, 2
OWNERS = ZN * XN
HEADS = 2
WIDTH = HEADS * HD
DM = 4096
PAIR = 2 * BLK
MEM = ("z", "x")
VMEM_LIMIT = 40 * 1024 * 1024
NEG_FILL = -1e30


def dot(a, b, dims):
    return lax.dot_general(a, b, (dims, ((), ())), preferred_element_type=jnp.float32)


def pick_kernel(asked_ref, block_ref, *out_refs):
    for head, out_ref in enumerate(out_refs):
        out_ref[...] = block_ref[:, :, :, head * HD : (head + 1) * HD]


def pick_blocks(asked, memory_kv):
    head_block = pl.BlockSpec((1, 2, BLK, HD), lambda i, asked_ref: (i, 0, 0, 0))
    return pl.pallas_call(
        pick_kernel,
        grid_spec=pltpu.PrefetchScalarGridSpec(
            num_scalar_prefetch=1,
            grid=(OWNERS,),
            in_specs=[
                pl.BlockSpec((1, 2, BLK, WIDTH), lambda i, asked_ref: (asked_ref[i], 0, 0, 0))
            ],
            out_specs=[head_block] * HEADS,
        ),
        out_shape=[jax.ShapeDtypeStruct((OWNERS, 2, BLK, HD), jnp.bfloat16)] * HEADS,
        compiler_params=pltpu.CompilerParams(vmem_limit_bytes=VMEM_LIMIT),
        cost_estimate=pl.CostEstimate(
            flops=0, bytes_accessed=2 * OWNERS * 2 * BLK * WIDTH * 2, transcendentals=0
        ),
        name="pick_blocks",
    )(asked, memory_kv)


def project_kernel(y_ref, x_ref, w_ref, *refs):
    out_refs, (rows_scr, acc_scr) = refs[:YN], refs[YN:]
    step = pl.program_id(0)
    x_index, y_index = step // YN, step % YN

    @pl.when(y_index == 0)
    def _():
        for z in range(ZN):
            start = pl.multiple_of((z * XN + x_index) * BLK, BLK)
            rows_scr[:, z * BLK : (z + 1) * BLK] = x_ref[:, pl.ds(start, BLK)]

    part = dot(rows_scr[...], w_ref[...].reshape(ZN * BLK, WIDTH), ((1,), (0,)))

    @pl.when(x_index == 0)
    def _():
        acc_scr[y_index] = part

    @pl.when(x_index > 0)
    def _():
        acc_scr[y_index] += part

    @pl.when(step == XN * YN - 1)
    def _():
        for shift, out_ref in enumerate(out_refs):
            out_ref[...] = acc_scr[lax.rem(y_ref[0] + shift, YN)].astype(jnp.bfloat16)


def project(y_index, rows, w_all):
    whole = pl.BlockSpec((PAIR, WIDTH), lambda i, y_ref: (0, 0))
    return pl.pallas_call(
        project_kernel,
        grid_spec=pltpu.PrefetchScalarGridSpec(
            num_scalar_prefetch=1,
            grid=(XN * YN,),
            in_specs=[
                pl.BlockSpec((PAIR, DM), lambda i, y_ref: (0, 0)),
                pl.BlockSpec((1, ZN, BLK, WIDTH), lambda i, y_ref: (i, 0, 0, 0)),
            ],
            out_specs=[whole] * YN,
            scratch_shapes=[
                pltpu.VMEM((PAIR, ZN * BLK), jnp.bfloat16),
                pltpu.VMEM((YN, PAIR, WIDTH), jnp.float32),
            ],
        ),
        out_shape=[jax.ShapeDtypeStruct((PAIR, WIDTH), jnp.bfloat16)] * YN,
        compiler_params=pltpu.CompilerParams(vmem_limit_bytes=VMEM_LIMIT),
        cost_estimate=pl.CostEstimate(
            flops=2 * PAIR * DM * YN * WIDTH,
            bytes_accessed=2 * (PAIR * DM + DM * YN * WIDTH + PAIR * YN * WIDTH),
            transcendentals=0,
        ),
        name="project",
    )(y_index, rows, w_all)


def attend_kernel(owner_ref, y_ref, *refs):
    query_refs, refs = refs[:YN], refs[YN:]
    local_ref, memory_ref, grad_ref = refs[:3]
    att_ref, out_refs, (query_scr, back_scr) = refs[-YN - 3], refs[-YN - 2 : -2], refs[-2:]
    y_index = y_ref[0]
    score_scale = 1.0 / math.sqrt(HD)
    for shift, query_ref in enumerate(query_refs):
        query_scr[lax.rem(y_index + YN - shift, YN)] = query_ref[...]
    row = lax.broadcasted_iota(jnp.int32, (BLK, BLK), 0)
    col = lax.broadcasted_iota(jnp.int32, (BLK, BLK), 1)
    causal = row >= col
    for tile in range(TILES):
        rows = slice(tile * BLK, (tile + 1) * BLK)
        half = slice(tile % 2 * BLK, (tile % 2 + 1) * BLK)
        query = query_scr[tile // 2, half, :]
        grad = grad_ref[rows, :]
        owners = [owner_ref[tile, slot] for slot in range(TOPK)]
        keys = jnp.concatenate(
            [memory_ref[owner, 0] for owner in owners] + [local_ref[0, : (tile + 1) * BLK, :]]
        )
        values = jnp.concatenate(
            [memory_ref[owner, 1] for owner in owners] + [local_ref[1, : (tile + 1) * BLK, :]]
        )
        scores = dot(query, keys, ((1,), (1,))) * score_scale
        scores = jnp.concatenate(
            [scores[:, :-BLK], jnp.where(causal, scores[:, -BLK:], NEG_FILL)], axis=1
        )
        dprobs = dot(grad, values, ((1,), (1,)))
        row_max = jnp.max(scores, axis=1, keepdims=True)
        exps = jnp.exp(scores - row_max)
        probs = exps * (1.0 / jnp.sum(exps, axis=1, keepdims=True))
        attended = dot(probs.astype(jnp.bfloat16), values, ((1,), (0,)))
        att_ref[rows, :] = attended.astype(jnp.bfloat16)
        delta = jnp.sum(probs * dprobs, axis=1, keepdims=True)
        dscores = (probs * (dprobs - delta)).astype(jnp.bfloat16)
        back = dot(dscores, keys, ((1,), (0,))) * score_scale
        back_scr[tile // 2, half, :] = back.astype(jnp.bfloat16)
    for shift, out_ref in enumerate(out_refs):
        out_ref[...] = back_scr[lax.rem(y_index + shift, YN)]


def attend(head, owner_of, y_index, queries, local_kv, received, grad_out, attended):
    head_rows = pl.BlockSpec((CTX, HD), lambda i, *_: (0, head))
    part = pl.BlockSpec((PAIR, HD), lambda i, *_: (0, 0))
    operands = [*queries, local_kv, received, grad_out]
    in_specs = [pl.BlockSpec((PAIR, HD), lambda i, *_: (0, head))] * YN + [
        pl.BlockSpec((2, CTX, HD), lambda i, *_: (0, 0, head)),
        pl.BlockSpec((OWNERS, 2, BLK, HD), lambda i, *_: (0, 0, 0, 0)),
        head_rows,
    ]
    aliases = {}
    if attended is not None:
        operands.append(attended)
        in_specs.append(pl.BlockSpec(memory_space=pl.ANY))
        aliases = {len(operands) + 1: 0}
    keys_count = TILES * (TOPK * BLK) + BLK * TILES * (TILES + 1) // 2
    return pl.pallas_call(
        attend_kernel,
        grid_spec=pltpu.PrefetchScalarGridSpec(
            num_scalar_prefetch=2,
            grid=(1,),
            in_specs=in_specs,
            out_specs=[head_rows] + [part] * YN,
            scratch_shapes=[
                pltpu.VMEM((YN, PAIR, HD), jnp.bfloat16),
                pltpu.VMEM((YN, PAIR, HD), jnp.bfloat16),
            ],
        ),
        out_shape=[jax.ShapeDtypeStruct((CTX, WIDTH), jnp.bfloat16)]
        + [jax.ShapeDtypeStruct((PAIR, HD), jnp.bfloat16)] * YN,
        input_output_aliases=aliases,
        compiler_params=pltpu.CompilerParams(vmem_limit_bytes=VMEM_LIMIT),
        cost_estimate=pl.CostEstimate(
            flops=8 * BLK * keys_count * HD,
            bytes_accessed=2 * (OWNERS * 2 * BLK * HD + 6 * CTX * HD),
            transcendentals=BLK * keys_count,
        ),
        name="attend",
    )(owner_of, y_index, *operands)


def back_kernel(pos_ref, *refs):
    grad_refs, (w_ref, own_ref, send_ref) = refs[: YN * HEADS], refs[YN * HEADS :]
    x_index = pl.program_id(0)
    y_index, core = pos_ref[0], pos_ref[1]
    for out_ref, first in ((own_ref, core * BLK), (send_ref, (1 - core) * BLK)):
        rows = pl.ds(pl.multiple_of(first, BLK), BLK)
        total = jnp.zeros((BLK, ZN * BLK), jnp.float32)
        for shift in range(YN):
            grad = jnp.concatenate(
                [grad_refs[head * YN + shift][rows, :] for head in range(HEADS)], axis=1
            )
            weight = w_ref[lax.rem(y_index + YN - shift, YN)].reshape(ZN * BLK, WIDTH)
            total += dot(grad, weight, ((1,), (1,)))
        total = total.astype(out_ref.dtype)
        for z in range(ZN):
            start = pl.multiple_of((z * XN + x_index) * BLK, BLK)
            out_ref[:, pl.ds(start, BLK)] = total[:, z * BLK : (z + 1) * BLK]


def back_project(position, grads, w_all):
    part = pl.BlockSpec((PAIR, HD), lambda i, pos_ref: (0, 0))
    whole = pl.BlockSpec((BLK, DM), lambda i, pos_ref: (0, 0))
    return pl.pallas_call(
        back_kernel,
        grid_spec=pltpu.PrefetchScalarGridSpec(
            num_scalar_prefetch=1,
            grid=(XN,),
            in_specs=[part] * (YN * HEADS)
            + [pl.BlockSpec((YN, ZN, BLK, WIDTH), lambda i, pos_ref: (i, 0, 0, 0))],
            out_specs=[whole, whole],
        ),
        out_shape=[
            jax.ShapeDtypeStruct((BLK, DM), jnp.float32),
            jax.ShapeDtypeStruct((BLK, DM), jnp.bfloat16),
        ],
        compiler_params=pltpu.CompilerParams(vmem_limit_bytes=VMEM_LIMIT),
        cost_estimate=pl.CostEstimate(
            flops=2 * PAIR * DM * YN * WIDTH,
            bytes_accessed=2 * (2 * PAIR * DM + DM * YN * WIDTH),
            transcendentals=0,
        ),
        name="back_project",
    )(position, *grads, w_all)


def shift_y(array, shift):
    if shift == 0:
        return array
    return lax.ppermute(array, "y", [(i, (i + shift) % YN) for i in range(YN)])


def local(layer_input, w_query, local_kv, memory_kv, memory_ids, grad_out):
    y_index = lax.axis_index("y").astype(jnp.int32).reshape(1)
    core = lax.axis_index("c").astype(jnp.int32).reshape(1)
    me = lax.axis_index(MEM).astype(jnp.int32)
    all_ids = lax.all_gather(memory_ids, MEM, axis=0, tiled=True)
    all_ids = all_ids.reshape(OWNERS, TILES * TOPK)
    asked = jnp.max(jnp.where(all_ids // MB_DEV == me, all_ids % MB_DEV, 0), axis=1)
    outgoing = pick_blocks(asked, memory_kv)
    received = [
        lax.all_to_all(part, MEM, split_axis=0, concat_axis=0, tiled=True) for part in outgoing
    ]
    w_all = lax.all_gather(lax.all_gather(w_query, "z"), ("x", "y"))
    rows = lax.all_gather(layer_input, "c", axis=0, tiled=True)
    queries = project(y_index, rows, w_all)
    queries = [shift_y(part, shift) for shift, part in enumerate(queries)]
    owner_of = memory_ids // MB_DEV
    attended, grads = None, []
    for head in range(HEADS):
        attended, *parts = attend(
            head, owner_of, y_index, queries, local_kv, received[head], grad_out, attended
        )
        grads += [shift_y(part, shift) for shift, part in enumerate(parts)]
    own, send = back_project(jnp.concatenate([y_index, core]), grads, w_all)
    other = lax.ppermute(send, "c", [(0, 1), (1, 0)])
    return (attended, (own + other.astype(jnp.float32)).astype(jnp.bfloat16))


def solution(mesh):
    torus = Mesh(mesh.devices.reshape(ZN, XN, YN, CN), ("z", "x", "y", "c"))
    in_specs = (
        P(("z", "x", "y", "c"), None),
        P(MEM, ("y", "c")),
        P(None, MEM, ("y", "c")),
        P(MEM, None, None, ("y", "c")),
        P(MEM, None),
        P(MEM, ("y", "c")),
    )
    out_specs = (P(MEM, ("y", "c")), P(("z", "x", "y", "c"), None))
    return jax.shard_map(local, mesh=torus, in_specs=in_specs, out_specs=out_specs, check_vma=False)
```

```python
import functools
import functools
import math

import jax
import jax.numpy as jnp
from jax import lax
from jax.experimental import pallas as pl
from jax.experimental.pallas import tpu as pltpu
from jax.sharding import Mesh
from jax.sharding import PartitionSpec as P

HD = 128
BLK = 128
TOPK = 4
MB_DEV = 16
CTX = 1024
TILES = CTX // BLK
ZN, XN, YN, CN = 8, 4, 4, 2
OWNERS = ZN * XN
HEADS = 2
WIDTH = HEADS * HD
DM = 4096
PAIR = 2 * BLK
MEM = ("z", "x")
VMEM_LIMIT = 40 * 1024 * 1024
NEG_FILL = -1e30


def dot(a, b, dims):
    return lax.dot_general(a, b, (dims, ((), ())), preferred_element_type=jnp.float32)


def pick_kernel(asked_ref, block_ref, out_ref):
    out_ref[...] = block_ref[...]


def pick_blocks(asked, memory_kv):
    block = (1, 2, BLK, WIDTH)
    return pl.pallas_call(
        pick_kernel,
        grid_spec=pltpu.PrefetchScalarGridSpec(
            num_scalar_prefetch=1,
            grid=(OWNERS,),
            in_specs=[pl.BlockSpec(block, lambda i, asked_ref: (asked_ref[i], 0, 0, 0))],
            out_specs=pl.BlockSpec(block, lambda i, asked_ref: (i, 0, 0, 0)),
        ),
        out_shape=jax.ShapeDtypeStruct((OWNERS, 2, BLK, WIDTH), jnp.bfloat16),
        compiler_params=pltpu.CompilerParams(vmem_limit_bytes=VMEM_LIMIT),
        cost_estimate=pl.CostEstimate(
            flops=0, bytes_accessed=2 * OWNERS * 2 * BLK * WIDTH * 2, transcendentals=0
        ),
        name="pick_blocks",
    )(asked, memory_kv)


def weight_of(pieces, shift):
    own, below, far_first, far_last, above = pieces
    if shift == 2:
        weight = jnp.concatenate([far_first[...], far_last[...]])
    else:
        weight = {0: own, 1: below, 3: above}[shift][...]
    return weight.reshape(ZN * BLK, WIDTH)


def column_of(z_index, x_index, shift):
    return pl.multiple_of((lax.rem(z_index + ZN - shift, ZN) * XN + x_index) * BLK, BLK)


def project_kernel(x_shift, pos_ref, x_ref, *refs):
    pieces, refs = refs[:5], refs[5:]
    first, last = x_shift == 0, x_shift == XN - 1
    total_ref = None if first else refs[0]
    out_refs, rows_scr = refs[0 if first else 1 : -1], refs[-1]
    z_index, x_index = pos_ref[0], lax.rem(pos_ref[1] + XN - x_shift, XN)
    for shift in range(ZN):
        columns = pl.ds(column_of(z_index, x_index, shift), BLK)
        rows_scr[:, shift * BLK : (shift + 1) * BLK] = x_ref[:, columns]
    for shift in range(YN):
        part = dot(rows_scr[...], weight_of(pieces, shift), ((1,), (0,)))
        if not first:
            part += total_ref[shift]
        if last:
            out_refs[shift][...] = part.astype(jnp.bfloat16)
        else:
            out_refs[0][shift] = part


def project(x_shift, position, rows, pieces, total):
    in_vmem = pl.BlockSpec(memory_space=pltpu.VMEM)
    operands = [rows, *pieces] + ([] if total is None else [total])
    if x_shift == XN - 1:
        out_shape = [jax.ShapeDtypeStruct((PAIR, WIDTH), jnp.bfloat16)] * YN
    else:
        out_shape = jax.ShapeDtypeStruct((YN, PAIR, WIDTH), jnp.float32)
    return pl.pallas_call(
        functools.partial(project_kernel, x_shift),
        in_specs=[pl.BlockSpec(memory_space=pltpu.SMEM)] + [in_vmem] * len(operands),
        out_specs=jax.tree.map(lambda _: in_vmem, out_shape),
        out_shape=out_shape,
        scratch_shapes=[pltpu.VMEM((PAIR, ZN * BLK), jnp.bfloat16)],
        compiler_params=pltpu.CompilerParams(vmem_limit_bytes=VMEM_LIMIT),
        cost_estimate=pl.CostEstimate(
            flops=2 * PAIR * ZN * BLK * YN * WIDTH,
            bytes_accessed=2 * (PAIR * DM + ZN * BLK * YN * WIDTH) + 8 * YN * PAIR * WIDTH,
            transcendentals=0,
        ),
        name="project",
    )(position, *operands)


def attend_kernel(owner_ref, pos_ref, *refs):
    query_refs, refs = refs[:YN], refs[YN:]
    local_ref, memory_ref, grad_ref, att_ref = refs[:4]
    out_refs, (query_scr, back_scr) = refs[4:-2], refs[-2:]
    y_index = pos_ref[2]
    score_scale = 1.0 / math.sqrt(HD)
    for shift, query_ref in enumerate(query_refs):
        query_scr[lax.rem(y_index + shift, YN)] = query_ref[...]
    row = lax.broadcasted_iota(jnp.int32, (BLK, BLK), 0)
    col = lax.broadcasted_iota(jnp.int32, (BLK, BLK), 1)
    causal = row >= col
    for tile in range(TILES):
        rows = slice(tile * BLK, (tile + 1) * BLK)
        half = slice(tile % 2 * BLK, (tile % 2 + 1) * BLK)
        owners = [owner_ref[tile, slot] for slot in range(TOPK)]
        for head in range(HEADS):
            feats = slice(head * HD, (head + 1) * HD)
            query = query_scr[tile // 2, half, feats]
            grad = grad_ref[rows, feats]
            keys, values = [
                jnp.concatenate(
                    [memory_ref[owner, kind, :, feats] for owner in owners]
                    + [local_ref[kind, : (tile + 1) * BLK, feats]]
                )
                for kind in range(2)
            ]
            scores = dot(query, keys, ((1,), (1,))) * score_scale
            scores = jnp.concatenate(
                [scores[:, :-BLK], jnp.where(causal, scores[:, -BLK:], NEG_FILL)], axis=1
            )
            dprobs = dot(grad, values, ((1,), (1,)))
            row_max = jnp.max(scores, axis=1, keepdims=True)
            exps = jnp.exp(scores - row_max)
            probs = exps * (1.0 / jnp.sum(exps, axis=1, keepdims=True))
            attended = dot(probs.astype(jnp.bfloat16), values, ((1,), (0,)))
            att_ref[rows, feats] = attended.astype(jnp.bfloat16)
            delta = jnp.sum(probs * dprobs, axis=1, keepdims=True)
            dscores = (probs * (dprobs - delta)).astype(jnp.bfloat16)
            back = dot(dscores, keys, ((1,), (0,))) * score_scale
            back_scr[tile // 2, half, feats] = back.astype(jnp.bfloat16)
    for shift, out_ref in enumerate(out_refs):
        out_ref[...] = back_scr[lax.rem(y_index + shift, YN)]


def attend(owner_of, position, queries, local_kv, received, grad_out):
    in_smem, in_vmem = (pl.BlockSpec(memory_space=space) for space in (pltpu.SMEM, pltpu.VMEM))
    keys_count = TILES * (TOPK * BLK) + BLK * TILES * (TILES + 1) // 2
    attended, *grads = pl.pallas_call(
        attend_kernel,
        in_specs=[in_smem] * 2 + [in_vmem] * (YN + 3),
        out_specs=[in_vmem] * (YN + 1),
        out_shape=[jax.ShapeDtypeStruct((CTX, WIDTH), jnp.bfloat16)]
        + [jax.ShapeDtypeStruct((PAIR, WIDTH), jnp.bfloat16)] * YN,
        scratch_shapes=[pltpu.VMEM((YN, PAIR, WIDTH), jnp.bfloat16)] * 2,
        compiler_params=pltpu.CompilerParams(vmem_limit_bytes=VMEM_LIMIT),
        cost_estimate=pl.CostEstimate(
            flops=8 * BLK * keys_count * WIDTH,
            bytes_accessed=2 * (OWNERS * 2 * BLK * WIDTH + 6 * CTX * WIDTH),
            transcendentals=BLK * keys_count * HEADS,
        ),
        name="attend",
    )(owner_of, position, *queries, local_kv, received, grad_out)
    return attended, grads


def back_kernel(pos_ref, *refs):
    grad_refs, piece_refs = refs[:YN], refs[YN : YN + 5 * XN]
    own_ref, send_ref = refs[YN + 5 * XN : YN + 5 * XN + 2]
    held, sems = refs[YN + 5 * XN + 2 : -1], refs[-1]
    copies = [
        pltpu.make_async_copy(piece, slot, sems.at[i])
        for i, (piece, slot) in enumerate(zip(piece_refs, held))
    ]
    for copy in copies:
        copy.start()
    z_index, core = pos_ref[0], pos_ref[3]
    own_rows = pl.ds(pl.multiple_of(core * BLK, BLK), BLK)
    send_rows = pl.ds(pl.multiple_of((1 - core) * BLK, BLK), BLK)
    for x_shift in range(XN):
        x_index = lax.rem(pos_ref[1] + XN - x_shift, XN)
        for copy in copies[x_shift * 5 : x_shift * 5 + 5]:
            copy.wait()
        pieces = held[x_shift * 5 : x_shift * 5 + 5]
        weights = [weight_of(pieces, shift) for shift in range(YN)]
        for out_ref, rows in ((send_ref, send_rows), (own_ref, own_rows)):
            total = jnp.zeros((BLK, ZN * BLK), jnp.float32)
            for shift in range(YN):
                total += dot(grad_refs[shift][rows, :], weights[shift], ((1,), (1,)))
            total = total.astype(out_ref.dtype)
            for shift in range(ZN):
                columns = pl.ds(column_of(z_index, x_index, shift), BLK)
                out_ref[:, columns] = total[:, shift * BLK : (shift + 1) * BLK]


def back_project(position, grads, pieces):
    in_vmem = pl.BlockSpec(memory_space=pltpu.VMEM)
    pieces = [piece for one_x in pieces for piece in one_x]
    return pl.pallas_call(
        back_kernel,
        in_specs=[pl.BlockSpec(memory_space=pltpu.SMEM)]
        + [in_vmem] * YN
        + [pl.BlockSpec(memory_space=pl.ANY)] * len(pieces),
        out_specs=[in_vmem] * 2,
        out_shape=[
            jax.ShapeDtypeStruct((BLK, DM), jnp.float32),
            jax.ShapeDtypeStruct((BLK, DM), jnp.bfloat16),
        ],
        scratch_shapes=[pltpu.VMEM(piece.shape, piece.dtype) for piece in pieces]
        + [pltpu.SemaphoreType.DMA((len(pieces),))],
        compiler_params=pltpu.CompilerParams(vmem_limit_bytes=VMEM_LIMIT),
        cost_estimate=pl.CostEstimate(
            flops=2 * PAIR * DM * YN * WIDTH,
            bytes_accessed=2 * (2 * PAIR * DM + DM * YN * WIDTH),
            transcendentals=0,
        ),
        name="back_project",
    )(position, *grads, *pieces)


def move(array, axis, count, shift):
    if shift % count == 0:
        return array
    return lax.ppermute(array, axis, [(i, (i + shift) % count) for i in range(count)])


def around_y(own):
    below, above = move(own, "y", YN, 1), move(own, "y", YN, -1)
    half = own.shape[0] // 2
    return [
        own,
        below,
        move(below[:half], "y", YN, 1),
        move(above[half:], "y", YN, -1),
        above,
    ]


def local(layer_input, w_query, local_kv, memory_kv, memory_ids, grad_out):
    position = jnp.stack([lax.axis_index(axis) for axis in ("z", "x", "y", "c")]).astype(jnp.int32)
    owner_of = memory_ids // MB_DEV
    owners = jnp.arange(OWNERS, dtype=jnp.int32)
    wanted = jnp.max(
        jnp.where(owner_of[:, :, None] == owners, (memory_ids % MB_DEV)[:, :, None], 0),
        axis=(0, 1),
    )
    asked = lax.all_to_all(wanted.reshape(OWNERS, 1), MEM, 0, 0, tiled=True)
    received = lax.all_to_all(pick_blocks(asked[:, 0], memory_kv), MEM, 0, 0, tiled=True)
    own = jnp.stack([move(w_query, "z", ZN, shift) for shift in range(ZN)])
    rows = lax.all_gather(layer_input, "c", axis=0, tiled=True)
    pieces = [around_y(move(own, "x", XN, shift)) for shift in range(XN)]
    queries = None
    for x_shift in range(XN):
        queries = project(x_shift, position, rows, pieces[x_shift], queries)
    queries = [move(part, "y", YN, -shift) for shift, part in enumerate(queries)]
    attended, grads = attend(owner_of, position, queries, local_kv, received, grad_out)
    grads = [move(part, "y", YN, shift) for shift, part in enumerate(grads)]
    own_part, send = back_project(position, grads, pieces)
    other = move(send, "c", CN, 1)
    return (attended, (own_part + other.astype(jnp.float32)).astype(jnp.bfloat16))


def solution(mesh):
    torus = Mesh(mesh.devices.reshape(ZN, XN, YN, CN), ("z", "x", "y", "c"))
    in_specs = (
        P(("z", "x", "y", "c"), None),
        P(MEM, ("y", "c")),
        P(None, MEM, ("y", "c")),
        P(MEM, None, None, ("y", "c")),
        P(MEM, None),
        P(MEM, ("y", "c")),
    )
    out_specs = (P(MEM, ("y", "c")), P(("z", "x", "y", "c"), None))
    return jax.shard_map(local, mesh=torus, in_specs=in_specs, out_specs=out_specs, check_vma=False)
```

```python
import functools
import functools
import math

import jax
import jax.numpy as jnp
from jax import lax
from jax.experimental import pallas as pl
from jax.experimental.pallas import tpu as pltpu
from jax.sharding import Mesh
from jax.sharding import PartitionSpec as P

HD = 128
BLK = 128
TOPK = 4
MB_DEV = 16
CTX = 1024
TILES = CTX // BLK
ZN, XN, YN, CN = 8, 4, 4, 2
OWNERS = ZN * XN
HEADS = 2
WIDTH = HEADS * HD
DM = 4096
PAIR = 2 * BLK
MEM = ("z", "x")
VMEM_LIMIT = 40 * 1024 * 1024
NEG_FILL = -1e30
SCALE = 1.0 / math.sqrt(HD)
FAR = (2, 1, 3)


def dot(a, b, dims):
    return lax.dot_general(a, b, (dims, ((), ())), preferred_element_type=jnp.float32)


def pick_kernel(asked_ref, block_ref, out_ref):
    out_ref[...] = block_ref[...]


def pick_blocks(asked, memory_kv):
    block = (1, 2, BLK, WIDTH)
    return pl.pallas_call(
        pick_kernel,
        grid_spec=pltpu.PrefetchScalarGridSpec(
            num_scalar_prefetch=1,
            grid=(OWNERS,),
            in_specs=[pl.BlockSpec(block, lambda i, asked_ref: (asked_ref[i], 0, 0, 0))],
            out_specs=pl.BlockSpec(block, lambda i, asked_ref: (i, 0, 0, 0)),
        ),
        out_shape=jax.ShapeDtypeStruct((OWNERS, 2, BLK, WIDTH), jnp.bfloat16),
        compiler_params=pltpu.CompilerParams(vmem_limit_bytes=VMEM_LIMIT),
        cost_estimate=pl.CostEstimate(
            flops=0, bytes_accessed=2 * OWNERS * 2 * BLK * WIDTH * 2, transcendentals=0
        ),
        name="pick_blocks",
    )(asked, memory_kv)


def weight_of(pieces, shift):
    own, below, far_first, far_last, above = pieces
    if shift == 2:
        weight = jnp.concatenate([far_first[...], far_last[...]])
    else:
        weight = {0: own, 1: below, 3: above}[shift][...]
    return weight.reshape(ZN * BLK, WIDTH)


def column_of(z_index, x_index, shift):
    return pl.multiple_of((lax.rem(z_index + ZN - shift, ZN) * XN + x_index) * BLK, BLK)


def project_kernel(x_shift, pos_ref, x_ref, *refs):
    pieces, refs = refs[:5], refs[5:]
    first, last = x_shift == 0, x_shift == XN - 1
    total_ref = None if first else refs[0]
    out_refs, rows_scr = refs[0 if first else 1 : -1], refs[-1]
    z_index, x_index = pos_ref[0], lax.rem(pos_ref[1] + XN - x_shift, XN)
    for shift in range(ZN):
        columns = pl.ds(column_of(z_index, x_index, shift), BLK)
        rows_scr[:, shift * BLK : (shift + 1) * BLK] = x_ref[:, columns]
    for shift in range(YN):
        part = dot(rows_scr[...], weight_of(pieces, shift), ((1,), (0,)))
        if not first:
            part += total_ref[shift]
        if last:
            out_refs[shift][...] = part.astype(jnp.bfloat16)
        else:
            out_refs[0][shift] = part


def project(x_shift, position, rows, pieces, total):
    in_vmem = pl.BlockSpec(memory_space=pltpu.VMEM)
    operands = [rows, *pieces] + ([] if total is None else [total])
    if x_shift == XN - 1:
        out_shape = [jax.ShapeDtypeStruct((PAIR, WIDTH), jnp.bfloat16)] * YN
    else:
        out_shape = jax.ShapeDtypeStruct((YN, PAIR, WIDTH), jnp.float32)
    return pl.pallas_call(
        functools.partial(project_kernel, x_shift),
        in_specs=[pl.BlockSpec(memory_space=pltpu.SMEM)] + [in_vmem] * len(operands),
        out_specs=jax.tree.map(lambda _: in_vmem, out_shape),
        out_shape=out_shape,
        scratch_shapes=[pltpu.VMEM((PAIR, ZN * BLK), jnp.bfloat16)],
        compiler_params=pltpu.CompilerParams(vmem_limit_bytes=VMEM_LIMIT),
        cost_estimate=pl.CostEstimate(
            flops=2 * PAIR * ZN * BLK * YN * WIDTH,
            bytes_accessed=2 * (PAIR * DM + ZN * BLK * YN * WIDTH) + 8 * YN * PAIR * WIDTH,
            transcendentals=0,
        ),
        name="project",
    )(position, *operands)


def attend_local_kernel(pos_ref, *refs):
    query_refs, (local_ref, grad_ref, sum_ref, slope_ref, base_ref, stat_ref, query_scr) = (
        refs[:YN],
        refs[YN:],
    )
    for shift, query_ref in enumerate(query_refs):
        query_scr[lax.rem(pos_ref[2] + shift, YN)] = query_ref[...]
    row = lax.broadcasted_iota(jnp.int32, (BLK, BLK), 0)
    col = lax.broadcasted_iota(jnp.int32, (BLK, BLK), 1)
    causal = row >= col
    for tile in range(TILES):
        rows = slice(tile * BLK, (tile + 1) * BLK)
        half = slice(tile % 2 * BLK, (tile % 2 + 1) * BLK)
        for head in range(HEADS):
            feats = slice(head * HD, (head + 1) * HD)
            query = query_scr[tile // 2, half, feats]
            keys, values = [local_ref[kind, : (tile + 1) * BLK, feats] for kind in range(2)]
            scores = dot(query, keys, ((1,), (1,))) * SCALE
            last = jnp.where(causal, scores[:, -BLK:], NEG_FILL)
            scores = jnp.concatenate([scores[:, :-BLK], last], axis=1) if tile else last
            dprobs = dot(grad_ref[rows, feats], values, ((1,), (1,)))
            row_max = jnp.max(scores, axis=1, keepdims=True)
            exps = jnp.exp(scores - row_max)
            total = jnp.sum(exps, axis=1, keepdims=True)
            delta = jnp.sum(exps * dprobs, axis=1, keepdims=True) / total
            weights = exps.astype(jnp.bfloat16)
            slopes = (exps * (dprobs - delta)).astype(jnp.bfloat16)
            sum_ref[rows, feats] = dot(weights, values, ((1,), (0,)))
            slope_ref[rows, feats] = dot(slopes, keys, ((1,), (0,)))
            base_ref[rows, feats] = dot(weights, keys, ((1,), (0,)))
            for i, stat in enumerate((row_max, total, delta)):
                stat_ref[rows, 3 * head + i : 3 * head + i + 1] = stat


def attend_local(position, queries, local_kv, grad_out):
    in_vmem = pl.BlockSpec(memory_space=pltpu.VMEM)
    keys_count = BLK * TILES * (TILES + 1) // 2
    return pl.pallas_call(
        attend_local_kernel,
        in_specs=[pl.BlockSpec(memory_space=pltpu.SMEM)] + [in_vmem] * (YN + 2),
        out_specs=[in_vmem] * 4,
        out_shape=[jax.ShapeDtypeStruct((CTX, WIDTH), jnp.float32)] * 3
        + [jax.ShapeDtypeStruct((CTX, BLK), jnp.float32)],
        scratch_shapes=[pltpu.VMEM((YN, PAIR, WIDTH), jnp.bfloat16)],
        compiler_params=pltpu.CompilerParams(vmem_limit_bytes=VMEM_LIMIT),
        cost_estimate=pl.CostEstimate(
            flops=10 * BLK * keys_count * WIDTH,
            bytes_accessed=2 * 12 * CTX * WIDTH,
            transcendentals=BLK * keys_count * HEADS,
        ),
        name="attend_local",
    )(position, *queries, local_kv, grad_out)


def attend_memory_kernel(shifts, owner_ref, pos_ref, *refs):
    count = len(shifts)
    query_refs, refs = refs[:count], refs[count:]
    memory_ref, grad_ref, sum_ref, slope_ref, base_ref, stat_ref = refs[:6]
    back_refs, other_refs = refs[-count:], refs[6:-count]
    if shifts == (0,):
        *done_refs, whole_ref = other_refs
        for shift, done_ref in zip(FAR, done_refs):
            group = lax.rem(pos_ref[2] + shift, YN)
            whole_ref[pl.ds(pl.multiple_of(group * PAIR, PAIR), PAIR), :] = done_ref[...]
    for i, shift in enumerate(shifts):
        group = lax.rem(pos_ref[2] + shift, YN)
        for part in range(PAIR // BLK):
            tile = group * (PAIR // BLK) + part
            rows = pl.ds(pl.multiple_of(tile * BLK, BLK), BLK)
            half = slice(part * BLK, (part + 1) * BLK)
            owners = [owner_ref[tile, slot] for slot in range(TOPK)]
            for head in range(HEADS):
                feats = slice(head * HD, (head + 1) * HD)
                keys, values = [
                    jnp.concatenate([memory_ref[owner, kind, :, feats] for owner in owners])
                    for kind in range(2)
                ]
                scores = dot(query_refs[i][half, feats], keys, ((1,), (1,))) * SCALE
                dprobs = dot(grad_ref[rows, feats], values, ((1,), (1,)))
                stats = stat_ref[rows, :]
                local_max, local_total, local_delta = [
                    stats[:, 3 * head + j : 3 * head + j + 1] for j in range(3)
                ]
                row_max = jnp.maximum(jnp.max(scores, axis=1, keepdims=True), local_max)
                exps = jnp.exp(scores - row_max)
                factor = jnp.exp(local_max - row_max)
                total = jnp.sum(exps, axis=1, keepdims=True) + factor * local_total
                inverse = 1.0 / total
                probs = exps * inverse
                factor *= inverse
                delta = (
                    jnp.sum(probs * dprobs, axis=1, keepdims=True)
                    + factor * local_total * local_delta
                )
                attended = factor * sum_ref[rows, feats] + dot(
                    probs.astype(jnp.bfloat16), values, ((1,), (0,))
                )
                dscores = (probs * (dprobs - delta)).astype(jnp.bfloat16)
                back = dot(dscores, keys, ((1,), (0,))) + factor * (
                    slope_ref[rows, feats] + (local_delta - delta) * base_ref[rows, feats]
                )
                back_refs[i][half, feats] = (back * SCALE).astype(jnp.bfloat16)
                attended = attended.astype(jnp.bfloat16)
                if shifts == (0,):
                    whole_ref[rows, feats] = attended
                else:
                    other_refs[i][half, feats] = attended


def attend_memory(shifts, owner_of, position, queries, received, grad_out, prepared, done):
    in_smem, in_vmem = (pl.BlockSpec(memory_space=space) for space in (pltpu.SMEM, pltpu.VMEM))
    count = len(shifts)
    part = jax.ShapeDtypeStruct((PAIR, WIDTH), jnp.bfloat16)
    whole = [jax.ShapeDtypeStruct((CTX, WIDTH), jnp.bfloat16)]
    operands = [*[queries[shift] for shift in shifts], received, grad_out, *prepared, *done]
    out_shape = (whole if done else [part] * count) + [part] * count
    keys_count = count * (PAIR // BLK) * TOPK * BLK
    outs = pl.pallas_call(
        functools.partial(attend_memory_kernel, shifts),
        in_specs=[in_smem] * 2 + [in_vmem] * len(operands),
        out_specs=[in_vmem] * len(out_shape),
        out_shape=out_shape,
        compiler_params=pltpu.CompilerParams(vmem_limit_bytes=VMEM_LIMIT),
        cost_estimate=pl.CostEstimate(
            flops=8 * BLK * keys_count * WIDTH,
            bytes_accessed=2 * 12 * CTX * WIDTH,
            transcendentals=BLK * keys_count * HEADS,
        ),
        name="attend_memory",
    )(owner_of, position, *operands)
    return outs[:-count], outs[-count:]


def back_kernel(pos_ref, *refs):
    grad_refs, piece_refs = refs[:YN], refs[YN : YN + 5 * XN]
    own_ref, send_ref = refs[YN + 5 * XN : YN + 5 * XN + 2]
    held, (total_scr, sems) = refs[YN + 5 * XN + 2 : -2], refs[-2:]
    copies = [
        pltpu.make_async_copy(piece, slot, sems.at[i])
        for i, (piece, slot) in enumerate(zip(piece_refs, held))
    ]
    for copy in copies:
        copy.start()
    z_index, core = pos_ref[0], pos_ref[3]
    own_rows = pl.ds(pl.multiple_of(core * BLK, BLK), BLK)
    send_rows = pl.ds(pl.multiple_of((1 - core) * BLK, BLK), BLK)
    for x_shift in range(XN):
        x_index = lax.rem(pos_ref[1] + XN - x_shift, XN)
        for copy in copies[x_shift * 5 : x_shift * 5 + 5]:
            copy.wait()
        pieces = held[x_shift * 5 : x_shift * 5 + 5]
        total = jnp.zeros((PAIR, ZN * BLK), jnp.float32)
        for shift in range(YN):
            total += dot(grad_refs[shift][...], weight_of(pieces, shift), ((1,), (1,)))
        total_scr[...] = total
        for out_ref, rows in ((send_ref, send_rows), (own_ref, own_rows)):
            for shift in range(ZN):
                columns = pl.ds(column_of(z_index, x_index, shift), BLK)
                part = total_scr[rows, shift * BLK : (shift + 1) * BLK]
                out_ref[:, columns] = part.astype(out_ref.dtype)


def back_project(position, grads, pieces):
    in_vmem = pl.BlockSpec(memory_space=pltpu.VMEM)
    pieces = [piece for one_x in pieces for piece in one_x]
    return pl.pallas_call(
        back_kernel,
        in_specs=[pl.BlockSpec(memory_space=pltpu.SMEM)]
        + [in_vmem] * YN
        + [pl.BlockSpec(memory_space=pl.ANY)] * len(pieces),
        out_specs=[in_vmem] * 2,
        out_shape=[
            jax.ShapeDtypeStruct((BLK, DM), jnp.float32),
            jax.ShapeDtypeStruct((BLK, DM), jnp.bfloat16),
        ],
        scratch_shapes=[pltpu.VMEM(piece.shape, piece.dtype) for piece in pieces]
        + [pltpu.VMEM((PAIR, ZN * BLK), jnp.float32), pltpu.SemaphoreType.DMA((len(pieces),))],
        compiler_params=pltpu.CompilerParams(vmem_limit_bytes=VMEM_LIMIT),
        cost_estimate=pl.CostEstimate(
            flops=2 * PAIR * DM * YN * WIDTH,
            bytes_accessed=2 * (2 * PAIR * DM + DM * YN * WIDTH),
            transcendentals=0,
        ),
        name="back_project",
    )(position, *grads, *pieces)


def move(array, axis, count, shift):
    if shift % count == 0:
        return array
    return lax.ppermute(array, axis, [(i, (i + shift) % count) for i in range(count)])


def around_y(own):
    below, above = move(own, "y", YN, 1), move(own, "y", YN, -1)
    half = own.shape[0] // 2
    return [
        own,
        below,
        move(below[:half], "y", YN, 1),
        move(above[half:], "y", YN, -1),
        above,
    ]


def local(layer_input, w_query, local_kv, memory_kv, memory_ids, grad_out):
    position = jnp.stack([lax.axis_index(axis) for axis in ("z", "x", "y", "c")]).astype(jnp.int32)
    owner_of = memory_ids // MB_DEV
    owners = jnp.arange(OWNERS, dtype=jnp.int32)
    wanted = jnp.max(
        jnp.where(owner_of[:, :, None] == owners, (memory_ids % MB_DEV)[:, :, None], 0),
        axis=(0, 1),
    )
    weights = [move(w_query, "z", ZN, shift) for shift in range(ZN)]
    asked = lax.all_to_all(wanted.reshape(OWNERS, 1), MEM, 0, 0, tiled=True)
    asked, weights = lax.optimization_barrier((asked, weights))
    received = lax.all_to_all(pick_blocks(asked[:, 0], memory_kv), MEM, 0, 0, tiled=True)
    own = jnp.stack(weights)
    rows = lax.all_gather(layer_input, "c", axis=0, tiled=True)
    pieces = [around_y(move(own, "x", XN, shift)) for shift in range(XN)]
    queries = None
    for x_shift in range(XN):
        queries = project(x_shift, position, rows, pieces[x_shift], queries)
    queries = [move(part, "y", YN, -shift) for shift, part in enumerate(queries)]
    prepared = attend_local(position, queries, local_kv, grad_out)
    done, far = attend_memory(FAR, owner_of, position, queries, received, grad_out, prepared, [])
    far = {shift: move(part, "y", YN, shift) for shift, part in zip(FAR, far)}
    (attended,), (near,) = attend_memory(
        (0,), owner_of, position, queries, received, grad_out, prepared, done
    )
    grads = [near, far[1], far[2], far[3]]
    own_part, send = back_project(position, grads, pieces)
    other = move(send, "c", CN, 1)
    return (attended, (own_part + other.astype(jnp.float32)).astype(jnp.bfloat16))


def solution(mesh):
    torus = Mesh(mesh.devices.reshape(ZN, XN, YN, CN), ("z", "x", "y", "c"))
    in_specs = (
        P(("z", "x", "y", "c"), None),
        P(MEM, ("y", "c")),
        P(None, MEM, ("y", "c")),
        P(MEM, None, None, ("y", "c")),
        P(MEM, None),
        P(MEM, ("y", "c")),
    )
    out_specs = (P(MEM, ("y", "c")), P(("z", "x", "y", "c"), None))
    return jax.shard_map(local, mesh=torus, in_specs=in_specs, out_specs=out_specs, check_vma=False)
```

```python
import functools
import functools
import math

import jax
import jax.numpy as jnp
from jax import lax
from jax.experimental import pallas as pl
from jax.experimental.pallas import tpu as pltpu
from jax.sharding import Mesh
from jax.sharding import PartitionSpec as P

HD = 128
BLK = 128
TOPK = 4
MB_DEV = 16
CTX = 1024
TILES = CTX // BLK
ZN, XN, YN, CN = 8, 4, 4, 2
OWNERS = ZN * XN
HEADS = 2
WIDTH = HEADS * HD
DM = 4096
PAIR = 2 * BLK
MEM = ("z", "x")
VMEM_LIMIT = 24 * 1024 * 1024
NEG_FILL = -1e30
SCALE = 1.0 / math.sqrt(HD)
FAR = (2, 1, 3)


def dot(a, b, dims):
    return lax.dot_general(a, b, (dims, ((), ())), preferred_element_type=jnp.float32)


def pick_kernel(asked_ref, memory_ref, out_ref, sems):
    copies = [
        pltpu.make_async_copy(memory_ref.at[asked_ref[i]], out_ref.at[i], sems.at[i])
        for i in range(OWNERS)
    ]
    for copy in copies:
        copy.start()
    for copy in copies:
        copy.wait()


def pick_blocks(asked, memory_kv):
    in_hbm = pl.BlockSpec(memory_space=pltpu.HBM)
    return pl.pallas_call(
        pick_kernel,
        in_specs=[pl.BlockSpec(memory_space=pltpu.SMEM), in_hbm],
        out_specs=in_hbm,
        out_shape=jax.ShapeDtypeStruct((OWNERS, 2, BLK, WIDTH), jnp.bfloat16),
        scratch_shapes=[pltpu.SemaphoreType.DMA((OWNERS,))],
        compiler_params=pltpu.CompilerParams(vmem_limit_bytes=VMEM_LIMIT),
        cost_estimate=pl.CostEstimate(
            flops=0, bytes_accessed=2 * OWNERS * 2 * BLK * WIDTH * 2, transcendentals=0
        ),
        name="pick_blocks",
    )(asked, memory_kv)


def weight_of(pieces, shift):
    own, below, far_first, far_last, above = pieces
    if shift == 2:
        weight = jnp.concatenate([far_first[...], far_last[...]])
    else:
        weight = {0: own, 1: below, 3: above}[shift][...]
    return weight.reshape(ZN * BLK, WIDTH)


def column_of(z_index, x_index, shift):
    return pl.multiple_of((lax.rem(z_index + ZN - shift, ZN) * XN + x_index) * BLK, BLK)


def project_kernel(pos_ref, x_ref, *refs):
    piece_refs, out_ref = refs[:XN], refs[XN]
    total = jnp.zeros((PAIR, WIDTH), jnp.float32)
    for x_shift in range(XN):
        x_index = lax.rem(pos_ref[1] + XN - x_shift, XN)
        rows = jnp.concatenate(
            [x_ref[:, pl.ds(column_of(pos_ref[0], x_index, shift), BLK)] for shift in range(ZN)],
            axis=1,
        )
        total += dot(rows, piece_refs[x_shift][...].reshape(ZN * BLK, WIDTH), ((1,), (0,)))
    out_ref[...] = total.astype(jnp.bfloat16)


def project(position, rows, weights):
    piece = pl.BlockSpec((ZN, BLK, WIDTH), lambda i, pos_ref: (0, 0, 0))
    return pl.pallas_call(
        project_kernel,
        grid_spec=pltpu.PrefetchScalarGridSpec(
            num_scalar_prefetch=1,
            grid=(CTX // PAIR,),
            in_specs=[pl.BlockSpec((PAIR, DM), lambda i, pos_ref: (i, 0))] + [piece] * XN,
            out_specs=pl.BlockSpec((PAIR, WIDTH), lambda i, pos_ref: (i, 0)),
        ),
        out_shape=jax.ShapeDtypeStruct((CTX, WIDTH), jnp.bfloat16),
        compiler_params=pltpu.CompilerParams(vmem_limit_bytes=VMEM_LIMIT),
        cost_estimate=pl.CostEstimate(
            flops=2 * CTX * DM * WIDTH,
            bytes_accessed=2 * (CTX * DM + DM * WIDTH + CTX * WIDTH),
            transcendentals=0,
        ),
        name="project",
    )(position, rows, *weights)


def attend_local_kernel(query_ref, local_ref, grad_ref, *out_refs):
    sum_ref, slope_ref, base_ref, stat_ref = out_refs
    row = lax.broadcasted_iota(jnp.int32, (BLK, BLK), 0)
    col = lax.broadcasted_iota(jnp.int32, (BLK, BLK), 1)
    causal = row >= col
    heads = range(HEADS)
    feats = [slice(head * HD, (head + 1) * HD) for head in heads]
    for tile in range(TILES):
        rows = slice(tile * BLK, (tile + 1) * BLK)
        seen = slice(0, (tile + 1) * BLK)
        scores = [dot(query_ref[rows, f], local_ref[0, seen, f], ((1,), (1,))) for f in feats]
        dprobs = [dot(grad_ref[rows, f], local_ref[1, seen, f], ((1,), (1,))) for f in feats]
        last = [jnp.where(causal, s[:, -BLK:] * SCALE, NEG_FILL) for s in scores]
        if tile:
            scores = [
                jnp.concatenate([scores[h][:, :-BLK] * SCALE, last[h]], axis=1) for h in heads
            ]
        else:
            scores = last
        row_max = [jnp.max(s, axis=1, keepdims=True) for s in scores]
        exps = [jnp.exp(scores[h] - row_max[h]) for h in heads]
        total = [jnp.sum(e, axis=1, keepdims=True) for e in exps]
        weights = [e.astype(jnp.bfloat16) for e in exps]
        for h in heads:
            sum_ref[rows, feats[h]] = dot(weights[h], local_ref[1, seen, feats[h]], ((1,), (0,)))
            base_ref[rows, feats[h]] = dot(weights[h], local_ref[0, seen, feats[h]], ((1,), (0,)))
        delta = [
            jnp.sum(exps[h] * dprobs[h], axis=1, keepdims=True) / total[h] for h in heads
        ]
        slopes = [(exps[h] * (dprobs[h] - delta[h])).astype(jnp.bfloat16) for h in heads]
        for h in heads:
            slope_ref[rows, feats[h]] = dot(slopes[h], local_ref[0, seen, feats[h]], ((1,), (0,)))
            for i, stat in enumerate((row_max[h], total[h], delta[h])):
                stat_ref[rows, 3 * h + i : 3 * h + i + 1] = stat


def attend_local(queries, local_kv, grad_out):
    in_vmem = pl.BlockSpec(memory_space=pltpu.VMEM)
    keys_count = BLK * TILES * (TILES + 1) // 2
    return pl.pallas_call(
        attend_local_kernel,
        in_specs=[in_vmem] * 3,
        out_specs=[in_vmem] * 4,
        out_shape=[jax.ShapeDtypeStruct((CTX, WIDTH), jnp.float32)] * 3
        + [jax.ShapeDtypeStruct((CTX, BLK), jnp.float32)],
        compiler_params=pltpu.CompilerParams(vmem_limit_bytes=VMEM_LIMIT),
        cost_estimate=pl.CostEstimate(
            flops=10 * BLK * keys_count * WIDTH,
            bytes_accessed=2 * 12 * CTX * WIDTH,
            transcendentals=BLK * keys_count * HEADS,
        ),
        name="attend_local",
    )(queries, local_kv, grad_out)


def attend_memory_kernel(shifts, owner_ref, pos_ref, *refs):
    count, parts = len(shifts), PAIR // BLK
    query_ref, grad_ref, sum_ref, slope_ref, base_ref, stat_ref, memory_ref = refs[:7]
    other_refs, back_refs = refs[7 : -count - 2], refs[-count - 2 : -2]
    held, sems = refs[-2:]
    groups = [lax.rem(pos_ref[2] + shift, YN) for shift in shifts]
    copies = [
        pltpu.make_async_copy(
            memory_ref.at[owner_ref[group * parts + part, slot]],
            held.at[i * parts + part, slot],
            sems.at[i * parts + part, slot],
        )
        for i, group in enumerate(groups)
        for part in range(parts)
        for slot in range(TOPK)
    ]
    for copy in copies:
        copy.start()
    if shifts == (0,):
        *done_refs, whole_ref = other_refs
        for shift, done_ref in zip(FAR, done_refs):
            group = lax.rem(pos_ref[2] + shift, YN)
            whole_ref[pl.ds(pl.multiple_of(group * PAIR, PAIR), PAIR), :] = done_ref[...]
    for i, group in enumerate(groups):
        for copy in copies[i * parts * TOPK : (i + 1) * parts * TOPK]:
            copy.wait()
        units = [(part, head) for part in range(parts) for head in range(HEADS)]
        every = range(len(units))
        rows = [
            pl.ds(pl.multiple_of(group * PAIR + part * BLK, BLK), BLK) for part, head in units
        ]
        feats = [slice(head * HD, (head + 1) * HD) for part, head in units]
        keys, values = [
            [
                held[i * parts + part, :, kind, :, feats[u]].reshape(TOPK * BLK, HD)
                for u, (part, head) in enumerate(units)
            ]
            for kind in range(2)
        ]
        scores = [dot(query_ref[rows[u], feats[u]], keys[u], ((1,), (1,))) * SCALE for u in every]
        dprobs = [dot(grad_ref[rows[u], feats[u]], values[u], ((1,), (1,))) for u in every]
        stats = [
            [stat_ref[rows[u], 3 * head + j : 3 * head + j + 1] for j in range(3)]
            for u, (part, head) in enumerate(units)
        ]
        row_max = [
            jnp.maximum(jnp.max(scores[u], axis=1, keepdims=True), stats[u][0]) for u in every
        ]
        exps = [jnp.exp(scores[u] - row_max[u]) for u in every]
        factor = [jnp.exp(stats[u][0] - row_max[u]) for u in every]
        inverse = [
            1.0 / (jnp.sum(exps[u], axis=1, keepdims=True) + factor[u] * stats[u][1])
            for u in every
        ]
        probs = [exps[u] * inverse[u] for u in every]
        factor = [factor[u] * inverse[u] for u in every]
        delta = [
            jnp.sum(probs[u] * dprobs[u], axis=1, keepdims=True)
            + factor[u] * stats[u][1] * stats[u][2]
            for u in every
        ]
        dscores = [(probs[u] * (dprobs[u] - delta[u])).astype(jnp.bfloat16) for u in every]
        for u, (part, head) in enumerate(units):
            half = slice(part * BLK, (part + 1) * BLK)
            back = dot(dscores[u], keys[u], ((1,), (0,))) + factor[u] * (
                slope_ref[rows[u], feats[u]]
                + (stats[u][2] - delta[u]) * base_ref[rows[u], feats[u]]
            )
            back_refs[i][half, feats[u]] = (back * SCALE).astype(jnp.bfloat16)
        for u, (part, head) in enumerate(units):
            half = slice(part * BLK, (part + 1) * BLK)
            attended = factor[u] * sum_ref[rows[u], feats[u]] + dot(
                probs[u].astype(jnp.bfloat16), values[u], ((1,), (0,))
            )
            attended = attended.astype(jnp.bfloat16)
            if shifts == (0,):
                whole_ref[rows[u], feats[u]] = attended
            else:
                other_refs[i][half, feats[u]] = attended


def attend_memory(shifts, owner_of, position, queries, received, grad_out, prepared, done):
    in_smem, in_vmem = (pl.BlockSpec(memory_space=space) for space in (pltpu.SMEM, pltpu.VMEM))
    count, tiles = len(shifts), len(shifts) * (PAIR // BLK)
    part = jax.ShapeDtypeStruct((PAIR, WIDTH), jnp.bfloat16)
    whole = [jax.ShapeDtypeStruct((CTX, WIDTH), jnp.bfloat16)]
    operands = [queries, grad_out, *prepared, received, *done]
    out_shape = (whole if done else [part] * count) + [part] * count
    keys_count = tiles * TOPK * BLK
    outs = pl.pallas_call(
        functools.partial(attend_memory_kernel, shifts),
        in_specs=[in_smem] * 2
        + [in_vmem] * 6
        + [pl.BlockSpec(memory_space=pl.ANY)]
        + [in_vmem] * len(done),
        out_specs=[in_vmem] * len(out_shape),
        out_shape=out_shape,
        scratch_shapes=[
            pltpu.VMEM((tiles, TOPK, 2, BLK, WIDTH), jnp.bfloat16),
            pltpu.SemaphoreType.DMA((tiles, TOPK)),
        ],
        compiler_params=pltpu.CompilerParams(vmem_limit_bytes=VMEM_LIMIT),
        cost_estimate=pl.CostEstimate(
            flops=8 * BLK * keys_count * WIDTH,
            bytes_accessed=2 * 12 * CTX * WIDTH,
            transcendentals=BLK * keys_count * HEADS,
        ),
        name="attend_memory",
    )(owner_of, position, *operands)
    return outs[:-count], outs[-count:]


def back_kernel(pos_ref, *refs):
    grad_refs, piece_refs = refs[:YN], refs[YN : YN + 5 * XN]
    own_ref, send_ref = refs[YN + 5 * XN : YN + 5 * XN + 2]
    held, (total_scr, sems) = refs[YN + 5 * XN + 2 : -2], refs[-2:]
    copies = [
        pltpu.make_async_copy(piece, slot, sems.at[i])
        for i, (piece, slot) in enumerate(zip(piece_refs, held))
    ]
    for copy in copies:
        copy.start()
    z_index, core = pos_ref[0], pos_ref[3]
    own_rows = pl.ds(pl.multiple_of(core * BLK, BLK), BLK)
    send_rows = pl.ds(pl.multiple_of((1 - core) * BLK, BLK), BLK)
    for x_shift in range(XN):
        x_index = lax.rem(pos_ref[1] + XN - x_shift, XN)
        for copy in copies[x_shift * 5 : x_shift * 5 + 5]:
            copy.wait()
        pieces = held[x_shift * 5 : x_shift * 5 + 5]
        total = jnp.zeros((PAIR, ZN * BLK), jnp.float32)
        for shift in range(YN):
            total += dot(grad_refs[shift][...], weight_of(pieces, shift), ((1,), (1,)))
        total_scr[...] = total
        for out_ref, rows in ((send_ref, send_rows), (own_ref, own_rows)):
            for shift in range(ZN):
                columns = pl.ds(column_of(z_index, x_index, shift), BLK)
                part = total_scr[rows, shift * BLK : (shift + 1) * BLK]
                out_ref[:, columns] = part.astype(out_ref.dtype)


def back_project(position, grads, pieces):
    in_vmem = pl.BlockSpec(memory_space=pltpu.VMEM)
    pieces = [piece for one_x in pieces for piece in one_x]
    return pl.pallas_call(
        back_kernel,
        in_specs=[pl.BlockSpec(memory_space=pltpu.SMEM)]
        + [in_vmem] * YN
        + [pl.BlockSpec(memory_space=pl.ANY)] * len(pieces),
        out_specs=[in_vmem] * 2,
        out_shape=[
            jax.ShapeDtypeStruct((BLK, DM), jnp.float32),
            jax.ShapeDtypeStruct((BLK, DM), jnp.bfloat16),
        ],
        scratch_shapes=[pltpu.VMEM(piece.shape, piece.dtype) for piece in pieces]
        + [pltpu.VMEM((PAIR, ZN * BLK), jnp.float32), pltpu.SemaphoreType.DMA((len(pieces),))],
        compiler_params=pltpu.CompilerParams(vmem_limit_bytes=VMEM_LIMIT),
        cost_estimate=pl.CostEstimate(
            flops=2 * PAIR * DM * YN * WIDTH,
            bytes_accessed=2 * (2 * PAIR * DM + DM * YN * WIDTH),
            transcendentals=0,
        ),
        name="back_project",
    )(position, *grads, *pieces)


def move(array, axis, count, shift):
    if shift % count == 0:
        return array
    return lax.ppermute(array, axis, [(i, (i + shift) % count) for i in range(count)])


def around_y(own):
    below, above = move(own, "y", YN, 1), move(own, "y", YN, -1)
    half = own.shape[0] // 2
    return [
        own,
        below,
        move(below[:half], "y", YN, 1),
        move(above[half:], "y", YN, -1),
        above,
    ]


def local(layer_input, w_query, local_kv, memory_kv, memory_ids, grad_out):
    position = jnp.stack([lax.axis_index(axis) for axis in ("z", "x", "y", "c")]).astype(jnp.int32)
    owner_of = memory_ids // MB_DEV
    owners = jnp.arange(OWNERS, dtype=jnp.int32)
    wanted = jnp.max(
        jnp.where(owner_of[:, :, None] == owners, (memory_ids % MB_DEV)[:, :, None], 0),
        axis=(0, 1),
    )
    weights = [move(w_query, "z", ZN, shift) for shift in range(ZN)]
    asked = lax.all_to_all(wanted.reshape(OWNERS, 1), MEM, 0, 0, tiled=True)
    asked, weights = lax.optimization_barrier((asked, weights))
    received = lax.all_to_all(pick_blocks(asked[:, 0], memory_kv), MEM, 0, 0, tiled=True)
    own = jnp.stack(weights)
    rows = lax.all_gather(layer_input, ("y", "c"), axis=0, tiled=True)
    columns = [move(own, "x", XN, shift) for shift in range(XN)]
    pieces = [around_y(part) for part in columns]
    queries = project(position, rows, columns)
    prepared = attend_local(queries, local_kv, grad_out)
    done, far = attend_memory(FAR, owner_of, position, queries, received, grad_out, prepared, [])
    far = {shift: move(part, "y", YN, shift) for shift, part in zip(FAR, far)}
    (attended,), (near,) = attend_memory(
        (0,), owner_of, position, queries, received, grad_out, prepared, done
    )
    grads = [near, far[1], far[2], far[3]]
    own_part, send = back_project(position, grads, pieces)
    other = move(send, "c", CN, 1)
    return (attended, (own_part + other.astype(jnp.float32)).astype(jnp.bfloat16))


def solution(mesh):
    torus = Mesh(mesh.devices.reshape(ZN, XN, YN, CN), ("z", "x", "y", "c"))
    in_specs = (
        P(("z", "x", "y", "c"), None),
        P(MEM, ("y", "c")),
        P(None, MEM, ("y", "c")),
        P(MEM, None, None, ("y", "c")),
        P(MEM, None),
        P(MEM, ("y", "c")),
    )
    out_specs = (P(MEM, ("y", "c")), P(("z", "x", "y", "c"), None))
    return jax.shard_map(local, mesh=torus, in_specs=in_specs, out_specs=out_specs, check_vma=False)
```

```python
import functools
import functools
import math

import jax
import jax.numpy as jnp
from jax import lax
from jax.experimental import pallas as pl
from jax.experimental.pallas import tpu as pltpu
from jax.sharding import Mesh
from jax.sharding import PartitionSpec as P

HD = 128
BLK = 128
TOPK = 4
MB_DEV = 16
CTX = 1024
TILES = CTX // BLK
ZN, XN, YN, CN = 8, 4, 4, 2
OWNERS = ZN * XN
HEADS = 2
WIDTH = HEADS * HD
DM = 4096
PAIR = 2 * BLK
MEM = ("z", "x")
MIB = 1024 * 1024
REST = (XN - 1) * ZN
NEG_FILL = -1e30
SCALE = 1.0 / math.sqrt(HD)
FAR = (2, 1, 3)


def dot(a, b, dims):
    return lax.dot_general(a, b, (dims, ((), ())), preferred_element_type=jnp.float32)


def pick_kernel(asked_ref, block_ref, out_ref):
    out_ref[...] = block_ref[...]


def pick_blocks(asked, memory_kv):
    block = (1, 2, BLK, WIDTH)
    return pl.pallas_call(
        pick_kernel,
        grid_spec=pltpu.PrefetchScalarGridSpec(
            num_scalar_prefetch=1,
            grid=(OWNERS,),
            in_specs=[pl.BlockSpec(block, lambda i, asked_ref: (asked_ref[i], 0, 0, 0))],
            out_specs=pl.BlockSpec(block, lambda i, asked_ref: (i, 0, 0, 0)),
        ),
        out_shape=jax.ShapeDtypeStruct((OWNERS, 2, BLK, WIDTH), jnp.bfloat16),
        compiler_params=pltpu.CompilerParams(vmem_limit_bytes=56 * MIB),
        cost_estimate=pl.CostEstimate(
            flops=0, bytes_accessed=2 * OWNERS * 2 * BLK * WIDTH * 2, transcendentals=0
        ),
        name="pick_blocks",
    )(asked, memory_kv)


def column_of(z_index, x_index, shift):
    return pl.multiple_of((lax.rem(z_index + ZN - shift, ZN) * XN + x_index) * BLK, BLK)


def project_kernel(pos_ref, x_ref, *refs):
    own_ref, rest_ref, out_ref = refs
    total = jnp.zeros((PAIR, WIDTH), jnp.float32)
    for x_shift in range(XN):
        x_index = lax.rem(pos_ref[1] + XN - x_shift, XN)
        rows = jnp.concatenate(
            [x_ref[:, pl.ds(column_of(pos_ref[0], x_index, shift), BLK)] for shift in range(ZN)],
            axis=1,
        )
        piece = rest_ref[(x_shift - 1) * ZN : x_shift * ZN] if x_shift else own_ref[...]
        total += dot(rows, piece.reshape(ZN * BLK, WIDTH), ((1,), (0,)))
    out_ref[...] = total.astype(jnp.bfloat16)


def project(position, rows, own, rest):
    pieces = [
        pl.BlockSpec((count, BLK, WIDTH), lambda i, pos_ref: (0, 0, 0)) for count in (ZN, REST)
    ]
    return pl.pallas_call(
        project_kernel,
        grid_spec=pltpu.PrefetchScalarGridSpec(
            num_scalar_prefetch=1,
            grid=(CTX // PAIR,),
            in_specs=[pl.BlockSpec((PAIR, DM), lambda i, pos_ref: (i, 0)), *pieces],
            out_specs=pl.BlockSpec((PAIR, WIDTH), lambda i, pos_ref: (i, 0)),
        ),
        out_shape=jax.ShapeDtypeStruct((CTX, WIDTH), jnp.bfloat16),
        compiler_params=pltpu.CompilerParams(vmem_limit_bytes=16 * MIB),
        cost_estimate=pl.CostEstimate(
            flops=2 * CTX * DM * WIDTH,
            bytes_accessed=2 * (CTX * DM + DM * WIDTH + CTX * WIDTH),
            transcendentals=0,
        ),
        name="project",
    )(position, rows, own, rest)


def attend_local_kernel(query_ref, local_ref, grad_ref, *out_refs):
    sum_ref, slope_ref, base_ref, stat_ref = out_refs
    row = lax.broadcasted_iota(jnp.int32, (BLK, BLK), 0)
    col = lax.broadcasted_iota(jnp.int32, (BLK, BLK), 1)
    causal = row >= col
    heads = range(HEADS)
    feats = [slice(head * HD, (head + 1) * HD) for head in heads]
    for tile in range(TILES):
        rows = slice(tile * BLK, (tile + 1) * BLK)
        seen = slice(0, (tile + 1) * BLK)
        scores = [dot(query_ref[rows, f], local_ref[0, seen, f], ((1,), (1,))) for f in feats]
        dprobs = [dot(grad_ref[rows, f], local_ref[1, seen, f], ((1,), (1,))) for f in feats]
        last = [jnp.where(causal, s[:, -BLK:] * SCALE, NEG_FILL) for s in scores]
        if tile:
            scores = [
                jnp.concatenate([scores[h][:, :-BLK] * SCALE, last[h]], axis=1) for h in heads
            ]
        else:
            scores = last
        row_max = [jnp.max(s, axis=1, keepdims=True) for s in scores]
        exps = [jnp.exp(scores[h] - row_max[h]) for h in heads]
        total = [jnp.sum(e, axis=1, keepdims=True) for e in exps]
        weights = [e.astype(jnp.bfloat16) for e in exps]
        for h in heads:
            part = dot(weights[h], local_ref[1, seen, feats[h]], ((1,), (0,)))
            sum_ref[rows, feats[h]] = part.astype(jnp.bfloat16)
            part = dot(weights[h], local_ref[0, seen, feats[h]], ((1,), (0,)))
            base_ref[rows, feats[h]] = part.astype(jnp.bfloat16)
        delta = [
            jnp.sum(exps[h] * dprobs[h], axis=1, keepdims=True) / total[h] for h in heads
        ]
        slopes = [(exps[h] * (dprobs[h] - delta[h])).astype(jnp.bfloat16) for h in heads]
        for h in heads:
            part = dot(slopes[h], local_ref[0, seen, feats[h]], ((1,), (0,)))
            slope_ref[rows, feats[h]] = part.astype(jnp.bfloat16)
            for i, stat in enumerate((row_max[h], total[h], delta[h])):
                stat_ref[rows, 3 * h + i : 3 * h + i + 1] = stat


def attend_local(queries, local_kv, grad_out):
    in_vmem = pl.BlockSpec(memory_space=pltpu.VMEM)
    keys_count = BLK * TILES * (TILES + 1) // 2
    return pl.pallas_call(
        attend_local_kernel,
        in_specs=[in_vmem] * 3,
        out_specs=[in_vmem] * 4,
        out_shape=[jax.ShapeDtypeStruct((CTX, WIDTH), jnp.bfloat16)] * 3
        + [jax.ShapeDtypeStruct((CTX, BLK), jnp.float32)],
        compiler_params=pltpu.CompilerParams(vmem_limit_bytes=10 * MIB),
        cost_estimate=pl.CostEstimate(
            flops=10 * BLK * keys_count * WIDTH,
            bytes_accessed=2 * 12 * CTX * WIDTH,
            transcendentals=BLK * keys_count * HEADS,
        ),
        name="attend_local",
    )(queries, local_kv, grad_out)


def attend_memory_kernel(shifts, owner_ref, pos_ref, *refs):
    count, parts = len(shifts), PAIR // BLK
    row_refs, memory_ref, refs = refs[:6], refs[6], refs[7:]
    row_scrs, (held, sems, row_sems), refs = refs[-9:-3], refs[-3:], refs[:-9]
    other_refs, back_refs = refs[:-count], refs[-count:]
    query_scr, grad_scr, sum_scr, slope_scr, base_scr, stat_scr = row_scrs
    groups = [lax.rem(pos_ref[2] + shift, YN) for shift in shifts]
    row_copies = [
        pltpu.make_async_copy(
            ref.at[pl.ds(pl.multiple_of(group * PAIR, PAIR), PAIR)], scr.at[i], row_sems.at[i, j]
        )
        for i, group in enumerate(groups)
        for j, (ref, scr) in enumerate(zip(row_refs, row_scrs))
    ]
    copies = [
        pltpu.make_async_copy(
            memory_ref.at[owner_ref[group * parts + part, slot]],
            held.at[i * parts + part, slot],
            sems.at[i * parts + part, slot],
        )
        for i, group in enumerate(groups)
        for part in range(parts)
        for slot in range(TOPK)
    ]
    for i in range(count):
        for copy in copies[i * parts * TOPK : (i + 1) * parts * TOPK]:
            copy.start()
        for copy in row_copies[i * 6 : i * 6 + 6]:
            copy.start()
    if shifts == (0,):
        *done_refs, whole_ref = other_refs
        for shift, done_ref in zip(FAR, done_refs):
            group = lax.rem(pos_ref[2] + shift, YN)
            whole_ref[pl.ds(pl.multiple_of(group * PAIR, PAIR), PAIR), :] = done_ref[...]
    for i, group in enumerate(groups):
        for copy in copies[i * parts * TOPK : (i + 1) * parts * TOPK]:
            copy.wait()
        for copy in row_copies[i * 6 : i * 6 + 6]:
            copy.wait()
        units = [(part, head) for part in range(parts) for head in range(HEADS)]
        every = range(len(units))
        rows = [slice(part * BLK, (part + 1) * BLK) for part, head in units]
        feats = [slice(head * HD, (head + 1) * HD) for part, head in units]
        keys, values = [
            [
                held[i * parts + part, :, kind, :, feats[u]].reshape(TOPK * BLK, HD)
                for u, (part, head) in enumerate(units)
            ]
            for kind in range(2)
        ]
        scores = [dot(query_scr[i, rows[u], feats[u]], keys[u], ((1,), (1,))) * SCALE for u in every]
        dprobs = [dot(grad_scr[i, rows[u], feats[u]], values[u], ((1,), (1,))) for u in every]
        stats = [
            [stat_scr[i, rows[u], 3 * head + j : 3 * head + j + 1] for j in range(3)]
            for u, (part, head) in enumerate(units)
        ]
        row_max = [
            jnp.maximum(jnp.max(scores[u], axis=1, keepdims=True), stats[u][0]) for u in every
        ]
        exps = [jnp.exp(scores[u] - row_max[u]) for u in every]
        factor = [jnp.exp(stats[u][0] - row_max[u]) for u in every]
        inverse = [
            1.0 / (jnp.sum(exps[u], axis=1, keepdims=True) + factor[u] * stats[u][1])
            for u in every
        ]
        delta = [
            inverse[u]
            * (
                jnp.sum(exps[u] * dprobs[u], axis=1, keepdims=True)
                + factor[u] * stats[u][1] * stats[u][2]
            )
            for u in every
        ]
        dscores = [(exps[u] * (dprobs[u] - delta[u])).astype(jnp.bfloat16) for u in every]
        for u, (part, head) in enumerate(units):
            back = dot(dscores[u], keys[u], ((1,), (0,))) + factor[u] * (
                slope_scr[i, rows[u], feats[u]].astype(jnp.float32)
                + (stats[u][2] - delta[u]) * base_scr[i, rows[u], feats[u]].astype(jnp.float32)
            )
            back_refs[i][rows[u], feats[u]] = (back * (inverse[u] * SCALE)).astype(jnp.bfloat16)
        for u, (part, head) in enumerate(units):
            attended = factor[u] * sum_scr[i, rows[u], feats[u]].astype(jnp.float32) + dot(
                exps[u].astype(jnp.bfloat16), values[u], ((1,), (0,))
            )
            attended = (attended * inverse[u]).astype(jnp.bfloat16)
            if shifts == (0,):
                whole_ref[pl.ds(pl.multiple_of(group * PAIR + part * BLK, BLK), BLK), feats[u]] = (
                    attended
                )
            else:
                other_refs[i][rows[u], feats[u]] = attended


def attend_memory(shifts, owner_of, position, queries, received, grad_out, prepared, done):
    in_smem, in_vmem = (pl.BlockSpec(memory_space=space) for space in (pltpu.SMEM, pltpu.VMEM))
    count, tiles = len(shifts), len(shifts) * (PAIR // BLK)
    part = jax.ShapeDtypeStruct((PAIR, WIDTH), jnp.bfloat16)
    whole = [jax.ShapeDtypeStruct((CTX, WIDTH), jnp.bfloat16)]
    operands = [queries, grad_out, *prepared, received, *done]
    out_shape = (whole if done else [part] * count) + [part] * count
    keys_count = tiles * TOPK * BLK
    outs = pl.pallas_call(
        functools.partial(attend_memory_kernel, shifts),
        in_specs=[in_smem] * 2
        + [pl.BlockSpec(memory_space=pl.ANY)] * 7
        + [in_vmem] * len(done),
        out_specs=[in_vmem] * len(out_shape),
        out_shape=out_shape,
        scratch_shapes=[pltpu.VMEM((count, PAIR, WIDTH), jnp.bfloat16)] * 5
        + [
            pltpu.VMEM((count, PAIR, BLK), jnp.float32),
            pltpu.VMEM((tiles, TOPK, 2, BLK, WIDTH), jnp.bfloat16),
            pltpu.SemaphoreType.DMA((tiles, TOPK)),
            pltpu.SemaphoreType.DMA((count, 6)),
        ],
        compiler_params=pltpu.CompilerParams(vmem_limit_bytes=58 * MIB),
        cost_estimate=pl.CostEstimate(
            flops=8 * BLK * keys_count * WIDTH,
            bytes_accessed=2 * 12 * CTX * WIDTH,
            transcendentals=BLK * keys_count * HEADS,
        ),
        name="attend_memory",
    )(owner_of, position, *operands)
    return outs[:-count], outs[-count:]


PLACES = (
    (0, 0, ZN),
    (1, 0, ZN),
    (2, 0, ZN),
    (3, 0, ZN),
    (0, ZN, REST),
    (1, ZN, REST),
    (2, ZN, REST // 2),
    (2, ZN + REST // 2, REST // 2),
    (3, ZN, REST),
)


def back_kernel(pos_ref, *refs):
    grad_refs, piece_refs = refs[:YN], refs[YN : YN + len(PLACES)]
    own_ref, send_ref, held, total_scr, sems = refs[YN + len(PLACES) :]
    copies = [
        pltpu.make_async_copy(piece, held.at[shift, pl.ds(first, count)], sems.at[i])
        for i, (piece, (shift, first, count)) in enumerate(zip(piece_refs, PLACES))
    ]
    for copy in copies:
        copy.start()
    core = pos_ref[3]
    own_rows = pl.ds(pl.multiple_of(core * BLK, BLK), BLK)
    send_rows = pl.ds(pl.multiple_of((1 - core) * BLK, BLK), BLK)
    for x_shift in range(XN):
        x_index = lax.rem(pos_ref[1] + XN - x_shift, XN)
        if x_shift < 2:
            for copy in copies[YN:] if x_shift else copies[:YN]:
                copy.wait()
        blocks = slice(x_shift * ZN, (x_shift + 1) * ZN)
        total = jnp.zeros((PAIR, ZN * BLK), jnp.float32)
        for shift in range(YN):
            weight = held[shift, blocks].reshape(ZN * BLK, WIDTH)
            total += dot(grad_refs[shift][...], weight, ((1,), (1,)))
        total_scr[...] = total
        for out_ref, rows in ((send_ref, send_rows), (own_ref, own_rows)):
            for shift in range(ZN):
                columns = pl.ds(column_of(pos_ref[0], x_index, shift), BLK)
                part = total_scr[rows, shift * BLK : (shift + 1) * BLK]
                out_ref[:, columns] = part.astype(out_ref.dtype)


def back_project(position, grads, pieces):
    in_vmem = pl.BlockSpec(memory_space=pltpu.VMEM)
    return pl.pallas_call(
        back_kernel,
        in_specs=[pl.BlockSpec(memory_space=pltpu.SMEM)]
        + [in_vmem] * YN
        + [pl.BlockSpec(memory_space=pl.ANY)] * len(pieces),
        out_specs=[in_vmem] * 2,
        out_shape=[
            jax.ShapeDtypeStruct((BLK, DM), jnp.float32),
            jax.ShapeDtypeStruct((BLK, DM), jnp.bfloat16),
        ],
        scratch_shapes=[
            pltpu.VMEM((YN, XN * ZN, BLK, WIDTH), jnp.bfloat16),
            pltpu.VMEM((PAIR, ZN * BLK), jnp.float32),
            pltpu.SemaphoreType.DMA((len(pieces),)),
        ],
        compiler_params=pltpu.CompilerParams(vmem_limit_bytes=20 * MIB),
        cost_estimate=pl.CostEstimate(
            flops=2 * PAIR * DM * YN * WIDTH,
            bytes_accessed=2 * (2 * PAIR * DM + DM * YN * WIDTH),
            transcendentals=0,
        ),
        name="back_project",
    )(position, *grads, *pieces)


def move(array, axis, count, shift):
    if shift % count == 0:
        return array
    return lax.ppermute(array, axis, [(i, (i + shift) % count) for i in range(count)])


def local(layer_input, w_query, local_kv, memory_kv, memory_ids, grad_out):
    position = jnp.stack([lax.axis_index(axis) for axis in ("z", "x", "y", "c")]).astype(jnp.int32)
    owner_of = memory_ids // MB_DEV
    owners = jnp.arange(OWNERS, dtype=jnp.int32)
    wanted = jnp.max(
        jnp.where(owner_of[:, :, None] == owners, (memory_ids % MB_DEV)[:, :, None], 0),
        axis=(0, 1),
    )
    weights = [move(w_query, "z", ZN, shift) for shift in range(ZN)]
    asked = lax.all_to_all(wanted.reshape(OWNERS, 1), MEM, 0, 0, tiled=True)
    asked, weights = lax.optimization_barrier((asked, weights))
    received = lax.all_to_all(pick_blocks(asked[:, 0], memory_kv), MEM, 0, 0, tiled=True)
    own = jnp.stack(weights)
    rows = lax.all_gather(layer_input, ("y", "c"), axis=0, tiled=True)
    rest = jnp.concatenate([move(own, "x", XN, shift) for shift in range(1, XN)])
    near_parts = [own, *[move(own, "y", YN, shift) for shift in range(1, YN)]]
    rest, near_parts = lax.optimization_barrier((rest, near_parts))
    below, above = move(rest, "y", YN, 1), move(rest, "y", YN, -1)
    queries = project(position, rows, own, rest)
    *sums, stats = attend_local(queries, local_kv, grad_out)
    below, above, stats = lax.optimization_barrier((below, above, stats))
    prepared = [*sums, stats]
    far_first = move(below[: REST // 2], "y", YN, 1)
    far_last = move(above[REST // 2 :], "y", YN, -1)
    pieces = [*near_parts, rest, below, far_first, far_last, above]
    done, far = attend_memory(FAR, owner_of, position, queries, received, grad_out, prepared, [])
    far = {shift: move(part, "y", YN, shift) for shift, part in zip(FAR, far)}
    (attended,), (near,) = attend_memory(
        (0,), owner_of, position, queries, received, grad_out, prepared, done
    )
    grads = [near, far[1], far[2], far[3]]
    own_part, send = back_project(position, grads, pieces)
    other = move(send, "c", CN, 1)
    return (attended, (own_part + other.astype(jnp.float32)).astype(jnp.bfloat16))


def solution(mesh):
    torus = Mesh(mesh.devices.reshape(ZN, XN, YN, CN), ("z", "x", "y", "c"))
    in_specs = (
        P(("z", "x", "y", "c"), None),
        P(MEM, ("y", "c")),
        P(None, MEM, ("y", "c")),
        P(MEM, None, None, ("y", "c")),
        P(MEM, None),
        P(MEM, ("y", "c")),
    )
    out_specs = (P(MEM, ("y", "c")), P(("z", "x", "y", "c"), None))
    return jax.shard_map(local, mesh=torus, in_specs=in_specs, out_specs=out_specs, check_vma=False)
```

```python
import functools
import functools
import math

import jax
import jax.numpy as jnp
from jax import lax
from jax.experimental import pallas as pl
from jax.experimental.pallas import tpu as pltpu
from jax.sharding import Mesh
from jax.sharding import PartitionSpec as P

HD = 128
BLK = 128
TOPK = 4
MB_DEV = 16
CTX = 1024
TILES = CTX // BLK
ZN, XN, YN, CN = 8, 4, 4, 2
OWNERS = ZN * XN
HEADS = 2
WIDTH = HEADS * HD
DM = 4096
PAIR = 2 * BLK
MEM = ("z", "x")
MIB = 1024 * 1024
REST = (XN - 1) * ZN
NEG_FILL = -1e30
SCALE = 1.0 / math.sqrt(HD)
FAR = (2, 1, 3)


def dot(a, b, dims):
    return lax.dot_general(a, b, (dims, ((), ())), preferred_element_type=jnp.float32)


def pick_kernel(asked_ref, block_ref, out_ref):
    out_ref[...] = block_ref[...]


def pick_blocks(asked, memory_kv):
    block = (1, 2, BLK, WIDTH)
    return pl.pallas_call(
        pick_kernel,
        grid_spec=pltpu.PrefetchScalarGridSpec(
            num_scalar_prefetch=1,
            grid=(OWNERS,),
            in_specs=[pl.BlockSpec(block, lambda i, asked_ref: (asked_ref[i], 0, 0, 0))],
            out_specs=pl.BlockSpec(block, lambda i, asked_ref: (i, 0, 0, 0)),
        ),
        out_shape=jax.ShapeDtypeStruct((OWNERS, 2, BLK, WIDTH), jnp.bfloat16),
        compiler_params=pltpu.CompilerParams(vmem_limit_bytes=4 * MIB),
        cost_estimate=pl.CostEstimate(
            flops=0, bytes_accessed=2 * OWNERS * 2 * BLK * WIDTH * 2, transcendentals=0
        ),
        name="pick_blocks",
    )(asked, memory_kv)


def column_of(z_index, x_index, shift):
    return pl.multiple_of((lax.rem(z_index + ZN - shift, ZN) * XN + x_index) * BLK, BLK)


def project_kernel(pos_ref, x_ref, *refs):
    own_ref, rest_ref, out_ref = refs
    total = jnp.zeros((PAIR, WIDTH), jnp.float32)
    for x_shift in range(XN):
        x_index = lax.rem(pos_ref[1] + XN - x_shift, XN)
        rows = jnp.concatenate(
            [x_ref[:, pl.ds(column_of(pos_ref[0], x_index, shift), BLK)] for shift in range(ZN)],
            axis=1,
        )
        piece = rest_ref[(x_shift - 1) * ZN : x_shift * ZN] if x_shift else own_ref[...]
        total += dot(rows, piece.reshape(ZN * BLK, WIDTH), ((1,), (0,)))
    out_ref[...] = total.astype(jnp.bfloat16)


def project(position, rows, own, rest):
    pieces = [
        pl.BlockSpec((count, BLK, WIDTH), lambda i, pos_ref: (0, 0, 0)) for count in (ZN, REST)
    ]
    return pl.pallas_call(
        project_kernel,
        grid_spec=pltpu.PrefetchScalarGridSpec(
            num_scalar_prefetch=1,
            grid=(CTX // PAIR,),
            in_specs=[pl.BlockSpec((PAIR, DM), lambda i, pos_ref: (i, 0)), *pieces],
            out_specs=pl.BlockSpec((PAIR, WIDTH), lambda i, pos_ref: (i, 0)),
        ),
        out_shape=jax.ShapeDtypeStruct((CTX, WIDTH), jnp.bfloat16),
        compiler_params=pltpu.CompilerParams(vmem_limit_bytes=16 * MIB),
        cost_estimate=pl.CostEstimate(
            flops=2 * CTX * DM * WIDTH,
            bytes_accessed=2 * (CTX * DM + DM * WIDTH + CTX * WIDTH),
            transcendentals=0,
        ),
        name="project",
    )(position, rows, own, rest)


def attend_local_kernel(query_ref, local_ref, grad_ref, *out_refs):
    sum_ref, slope_ref, base_ref, stat_ref = out_refs
    row = lax.broadcasted_iota(jnp.int32, (BLK, BLK), 0)
    col = lax.broadcasted_iota(jnp.int32, (BLK, BLK), 1)
    causal = row >= col
    heads = range(HEADS)
    feats = [slice(head * HD, (head + 1) * HD) for head in heads]
    for tile in range(TILES):
        rows = slice(tile * BLK, (tile + 1) * BLK)
        seen = slice(0, (tile + 1) * BLK)
        scores = [dot(query_ref[rows, f], local_ref[0, seen, f], ((1,), (1,))) for f in feats]
        dprobs = [dot(grad_ref[rows, f], local_ref[1, seen, f], ((1,), (1,))) for f in feats]
        last = [jnp.where(causal, s[:, -BLK:] * SCALE, NEG_FILL) for s in scores]
        if tile:
            scores = [
                jnp.concatenate([scores[h][:, :-BLK] * SCALE, last[h]], axis=1) for h in heads
            ]
        else:
            scores = last
        row_max = [jnp.max(s, axis=1, keepdims=True) for s in scores]
        exps = [jnp.exp(scores[h] - row_max[h]) for h in heads]
        total = [jnp.sum(e, axis=1, keepdims=True) for e in exps]
        weights = [e.astype(jnp.bfloat16) for e in exps]
        for h in heads:
            part = dot(weights[h], local_ref[1, seen, feats[h]], ((1,), (0,)))
            sum_ref[rows, feats[h]] = part.astype(jnp.bfloat16)
            part = dot(weights[h], local_ref[0, seen, feats[h]], ((1,), (0,)))
            base_ref[rows, feats[h]] = part.astype(jnp.bfloat16)
        delta = [
            jnp.sum(exps[h] * dprobs[h], axis=1, keepdims=True) / total[h] for h in heads
        ]
        slopes = [(exps[h] * (dprobs[h] - delta[h])).astype(jnp.bfloat16) for h in heads]
        for h in heads:
            part = dot(slopes[h], local_ref[0, seen, feats[h]], ((1,), (0,)))
            slope_ref[rows, feats[h]] = part.astype(jnp.bfloat16)
            for i, stat in enumerate((row_max[h], total[h], delta[h])):
                stat_ref[rows, 3 * h + i : 3 * h + i + 1] = stat


def attend_local(queries, local_kv, grad_out):
    in_vmem = pl.BlockSpec(memory_space=pltpu.VMEM)
    keys_count = BLK * TILES * (TILES + 1) // 2
    return pl.pallas_call(
        attend_local_kernel,
        in_specs=[in_vmem] * 3,
        out_specs=[in_vmem] * 4,
        out_shape=[jax.ShapeDtypeStruct((CTX, WIDTH), jnp.bfloat16)] * 3
        + [jax.ShapeDtypeStruct((CTX, BLK), jnp.float32)],
        compiler_params=pltpu.CompilerParams(vmem_limit_bytes=10 * MIB),
        cost_estimate=pl.CostEstimate(
            flops=10 * BLK * keys_count * WIDTH,
            bytes_accessed=2 * 12 * CTX * WIDTH,
            transcendentals=BLK * keys_count * HEADS,
        ),
        name="attend_local",
    )(queries, local_kv, grad_out)


def attend_memory_kernel(shifts, owner_ref, pos_ref, *refs):
    count, parts = len(shifts), PAIR // BLK
    row_refs, memory_ref, refs = refs[:6], refs[6], refs[7:]
    row_scrs, (held, sems, row_sems), refs = refs[-9:-3], refs[-3:], refs[:-9]
    other_refs, back_refs = refs[:-count], refs[-count:]
    query_scr, grad_scr, sum_scr, slope_scr, base_scr, stat_scr = row_scrs
    groups = [lax.rem(pos_ref[2] + shift, YN) for shift in shifts]
    row_copies = [
        pltpu.make_async_copy(
            ref.at[pl.ds(pl.multiple_of(group * PAIR, PAIR), PAIR)], scr.at[i], row_sems.at[i, j]
        )
        for i, group in enumerate(groups)
        for j, (ref, scr) in enumerate(zip(row_refs, row_scrs))
    ]
    copies = [
        pltpu.make_async_copy(
            memory_ref.at[owner_ref[group * parts + part, slot]],
            held.at[i * parts + part, slot],
            sems.at[i * parts + part, slot],
        )
        for i, group in enumerate(groups)
        for part in range(parts)
        for slot in range(TOPK)
    ]
    for i in range(count):
        for copy in copies[i * parts * TOPK : (i + 1) * parts * TOPK]:
            copy.start()
        for copy in row_copies[i * 6 : i * 6 + 6]:
            copy.start()
    if shifts == (0,):
        *done_refs, whole_ref = other_refs
        for shift, done_ref in zip(FAR, done_refs):
            group = lax.rem(pos_ref[2] + shift, YN)
            whole_ref[pl.ds(pl.multiple_of(group * PAIR, PAIR), PAIR), :] = done_ref[...]
    for i, group in enumerate(groups):
        for copy in copies[i * parts * TOPK : (i + 1) * parts * TOPK]:
            copy.wait()
        for copy in row_copies[i * 6 : i * 6 + 6]:
            copy.wait()
        units = [(part, head) for part in range(parts) for head in range(HEADS)]
        every = range(len(units))
        rows = [slice(part * BLK, (part + 1) * BLK) for part, head in units]
        feats = [slice(head * HD, (head + 1) * HD) for part, head in units]
        keys, values = [
            [
                held[i * parts + part, :, kind, :, feats[u]].reshape(TOPK * BLK, HD)
                for u, (part, head) in enumerate(units)
            ]
            for kind in range(2)
        ]
        scores = [dot(query_scr[i, rows[u], feats[u]], keys[u], ((1,), (1,))) * SCALE for u in every]
        dprobs = [dot(grad_scr[i, rows[u], feats[u]], values[u], ((1,), (1,))) for u in every]
        stats = [
            [stat_scr[i, rows[u], 3 * head + j : 3 * head + j + 1] for j in range(3)]
            for u, (part, head) in enumerate(units)
        ]
        row_max = [
            jnp.maximum(jnp.max(scores[u], axis=1, keepdims=True), stats[u][0]) for u in every
        ]
        exps = [jnp.exp(scores[u] - row_max[u]) for u in every]
        factor = [jnp.exp(stats[u][0] - row_max[u]) for u in every]
        inverse = [
            1.0 / (jnp.sum(exps[u], axis=1, keepdims=True) + factor[u] * stats[u][1])
            for u in every
        ]
        delta = [
            inverse[u]
            * (
                jnp.sum(exps[u] * dprobs[u], axis=1, keepdims=True)
                + factor[u] * stats[u][1] * stats[u][2]
            )
            for u in every
        ]
        dscores = [(exps[u] * (dprobs[u] - delta[u])).astype(jnp.bfloat16) for u in every]
        for u, (part, head) in enumerate(units):
            back = dot(dscores[u], keys[u], ((1,), (0,))) + factor[u] * (
                slope_scr[i, rows[u], feats[u]].astype(jnp.float32)
                + (stats[u][2] - delta[u]) * base_scr[i, rows[u], feats[u]].astype(jnp.float32)
            )
            back_refs[i][rows[u], feats[u]] = (back * (inverse[u] * SCALE)).astype(jnp.bfloat16)
        for u, (part, head) in enumerate(units):
            attended = factor[u] * sum_scr[i, rows[u], feats[u]].astype(jnp.float32) + dot(
                exps[u].astype(jnp.bfloat16), values[u], ((1,), (0,))
            )
            attended = (attended * inverse[u]).astype(jnp.bfloat16)
            if shifts == (0,):
                whole_ref[pl.ds(pl.multiple_of(group * PAIR + part * BLK, BLK), BLK), feats[u]] = (
                    attended
                )
            else:
                other_refs[i][rows[u], feats[u]] = attended


def attend_memory(shifts, owner_of, position, queries, received, grad_out, prepared, done):
    in_smem, in_vmem = (pl.BlockSpec(memory_space=space) for space in (pltpu.SMEM, pltpu.VMEM))
    count, tiles = len(shifts), len(shifts) * (PAIR // BLK)
    part = jax.ShapeDtypeStruct((PAIR, WIDTH), jnp.bfloat16)
    whole = [jax.ShapeDtypeStruct((CTX, WIDTH), jnp.bfloat16)]
    operands = [queries, grad_out, *prepared, received, *done]
    out_shape = (whole if done else [part] * count) + [part] * count
    keys_count = tiles * TOPK * BLK
    outs = pl.pallas_call(
        functools.partial(attend_memory_kernel, shifts),
        in_specs=[in_smem] * 2
        + [pl.BlockSpec(memory_space=pl.ANY)] * 7
        + [in_vmem] * len(done),
        out_specs=[in_vmem] * len(out_shape),
        out_shape=out_shape,
        scratch_shapes=[pltpu.VMEM((count, PAIR, WIDTH), jnp.bfloat16)] * 5
        + [
            pltpu.VMEM((count, PAIR, BLK), jnp.float32),
            pltpu.VMEM((tiles, TOPK, 2, BLK, WIDTH), jnp.bfloat16),
            pltpu.SemaphoreType.DMA((tiles, TOPK)),
            pltpu.SemaphoreType.DMA((count, 6)),
        ],
        compiler_params=pltpu.CompilerParams(vmem_limit_bytes=58 * MIB),
        cost_estimate=pl.CostEstimate(
            flops=8 * BLK * keys_count * WIDTH,
            bytes_accessed=2 * 12 * CTX * WIDTH,
            transcendentals=BLK * keys_count * HEADS,
        ),
        name="attend_memory",
    )(owner_of, position, *operands)
    return outs[:-count], outs[-count:]


PLACES = (
    (0, 0, ZN),
    (1, 0, ZN),
    (2, 0, ZN),
    (3, 0, ZN),
    (0, ZN, REST),
    (1, ZN, REST),
    (2, ZN, REST // 2),
    (2, ZN + REST // 2, REST // 2),
    (3, ZN, REST),
)


def back_kernel(pos_ref, *refs):
    grad_refs, piece_refs = refs[:YN], refs[YN : YN + len(PLACES)]
    own_ref, send_ref, held, total_scr, sems = refs[YN + len(PLACES) :]
    copies = [
        pltpu.make_async_copy(piece, held.at[shift, pl.ds(first, count)], sems.at[i])
        for i, (piece, (shift, first, count)) in enumerate(zip(piece_refs, PLACES))
    ]
    for copy in copies:
        copy.start()
    core = pos_ref[3]
    own_rows = pl.ds(pl.multiple_of(core * BLK, BLK), BLK)
    send_rows = pl.ds(pl.multiple_of((1 - core) * BLK, BLK), BLK)
    for x_shift in range(XN):
        x_index = lax.rem(pos_ref[1] + XN - x_shift, XN)
        if x_shift < 2:
            for copy in copies[YN:] if x_shift else copies[:YN]:
                copy.wait()
        blocks = slice(x_shift * ZN, (x_shift + 1) * ZN)
        total = jnp.zeros((PAIR, ZN * BLK), jnp.float32)
        for shift in range(YN):
            weight = held[shift, blocks].reshape(ZN * BLK, WIDTH)
            total += dot(grad_refs[shift][...], weight, ((1,), (1,)))
        total_scr[...] = total
        for out_ref, rows in ((send_ref, send_rows), (own_ref, own_rows)):
            for shift in range(ZN):
                columns = pl.ds(column_of(pos_ref[0], x_index, shift), BLK)
                part = total_scr[rows, shift * BLK : (shift + 1) * BLK]
                out_ref[:, columns] = part.astype(out_ref.dtype)


def back_project(position, grads, pieces):
    in_vmem = pl.BlockSpec(memory_space=pltpu.VMEM)
    return pl.pallas_call(
        back_kernel,
        in_specs=[pl.BlockSpec(memory_space=pltpu.SMEM)]
        + [in_vmem] * YN
        + [pl.BlockSpec(memory_space=pl.ANY)] * len(pieces),
        out_specs=[in_vmem] * 2,
        out_shape=[
            jax.ShapeDtypeStruct((BLK, DM), jnp.float32),
            jax.ShapeDtypeStruct((BLK, DM), jnp.bfloat16),
        ],
        scratch_shapes=[
            pltpu.VMEM((YN, XN * ZN, BLK, WIDTH), jnp.bfloat16),
            pltpu.VMEM((PAIR, ZN * BLK), jnp.float32),
            pltpu.SemaphoreType.DMA((len(pieces),)),
        ],
        compiler_params=pltpu.CompilerParams(vmem_limit_bytes=20 * MIB),
        cost_estimate=pl.CostEstimate(
            flops=2 * PAIR * DM * YN * WIDTH,
            bytes_accessed=2 * (2 * PAIR * DM + DM * YN * WIDTH),
            transcendentals=0,
        ),
        name="back_project",
    )(position, *grads, *pieces)


def move(array, axis, count, shift):
    if shift % count == 0:
        return array
    return lax.ppermute(array, axis, [(i, (i + shift) % count) for i in range(count)])


def local(layer_input, w_query, local_kv, memory_kv, memory_ids, grad_out):
    position = jnp.stack([lax.axis_index(axis) for axis in ("z", "x", "y", "c")]).astype(jnp.int32)
    owner_of = memory_ids // MB_DEV
    owners = jnp.arange(OWNERS, dtype=jnp.int32)
    wanted = jnp.max(
        jnp.where(owner_of[:, :, None] == owners, (memory_ids % MB_DEV)[:, :, None], 0),
        axis=(0, 1),
    )
    weights = [move(w_query, "z", ZN, shift) for shift in range(ZN)]
    asked = lax.all_to_all(wanted.reshape(OWNERS, 1), MEM, 0, 0, tiled=True)
    asked, weights = lax.optimization_barrier((asked, weights))
    received = lax.all_to_all(pick_blocks(asked[:, 0], memory_kv), MEM, 0, 0, tiled=True)
    own = jnp.stack(weights)
    rows = lax.all_gather(layer_input, ("y", "c"), axis=0, tiled=True)
    rest = jnp.concatenate([move(own, "x", XN, shift) for shift in range(1, XN)])
    near_parts = [own, *[move(own, "y", YN, shift) for shift in range(1, YN)]]
    rest, near_parts = lax.optimization_barrier((rest, near_parts))
    below, above = move(rest, "y", YN, 1), move(rest, "y", YN, -1)
    queries = project(position, rows, own, rest)
    *sums, stats = attend_local(queries, local_kv, grad_out)
    below, above, stats = lax.optimization_barrier((below, above, stats))
    prepared = [*sums, stats]
    far_first = move(below[: REST // 2], "y", YN, 1)
    far_last = move(above[REST // 2 :], "y", YN, -1)
    pieces = [*near_parts, rest, below, far_first, far_last, above]
    done, far = attend_memory(FAR, owner_of, position, queries, received, grad_out, prepared, [])
    far = {shift: move(part, "y", YN, shift) for shift, part in zip(FAR, far)}
    (attended,), (near,) = attend_memory(
        (0,), owner_of, position, queries, received, grad_out, prepared, done
    )
    grads = [near, far[1], far[2], far[3]]
    own_part, send = back_project(position, grads, pieces)
    other = move(send, "c", CN, 1)
    return (attended, (own_part + other.astype(jnp.float32)).astype(jnp.bfloat16))


def solution(mesh):
    torus = Mesh(mesh.devices.reshape(ZN, XN, YN, CN), ("z", "x", "y", "c"))
    in_specs = (
        P(("z", "x", "y", "c"), None),
        P(MEM, ("y", "c")),
        P(None, MEM, ("y", "c")),
        P(MEM, None, None, ("y", "c")),
        P(MEM, None),
        P(MEM, ("y", "c")),
    )
    out_specs = (P(MEM, ("y", "c")), P(("z", "x", "y", "c"), None))
    return jax.shard_map(local, mesh=torus, in_specs=in_specs, out_specs=out_specs, check_vma=False)
```

```python
import functools
import functools
import math

import jax
import jax.numpy as jnp
from jax import lax
from jax.experimental import pallas as pl
from jax.experimental.pallas import tpu as pltpu
from jax.sharding import Mesh
from jax.sharding import PartitionSpec as P

HD = 128
BLK = 128
TOPK = 4
MB_DEV = 16
CTX = 1024
TILES = CTX // BLK
ZN, XN, YN, CN = 8, 4, 4, 2
OWNERS = ZN * XN
HEADS = 2
WIDTH = HEADS * HD
DM = 4096
PAIR = 2 * BLK
MEM = ("z", "x")
MIB = 1024 * 1024
HALF = (XN - 1) * ZN // 2
NEG_FILL = -1e30
SCALE = 1.0 / math.sqrt(HD)
FAR = (2, 1, 3)


def dot(a, b, dims):
    return lax.dot_general(a, b, (dims, ((), ())), preferred_element_type=jnp.float32)


def pick_kernel(asked_ref, block_ref, out_ref):
    out_ref[...] = block_ref[...]


def pick_blocks(asked, memory_kv):
    block = (1, 2, BLK, WIDTH)
    return pl.pallas_call(
        pick_kernel,
        grid_spec=pltpu.PrefetchScalarGridSpec(
            num_scalar_prefetch=1,
            grid=(OWNERS,),
            in_specs=[pl.BlockSpec(block, lambda i, asked_ref: (asked_ref[i], 0, 0, 0))],
            out_specs=pl.BlockSpec(block, lambda i, asked_ref: (i, 0, 0, 0)),
        ),
        out_shape=jax.ShapeDtypeStruct((OWNERS, 2, BLK, WIDTH), jnp.bfloat16),
        compiler_params=pltpu.CompilerParams(vmem_limit_bytes=4 * MIB),
        cost_estimate=pl.CostEstimate(
            flops=0, bytes_accessed=2 * OWNERS * 2 * BLK * WIDTH * 2, transcendentals=0
        ),
        name="pick_blocks",
    )(asked, memory_kv)


def column_of(z_index, x_index, shift):
    return pl.multiple_of((lax.rem(z_index + ZN - shift, ZN) * XN + x_index) * BLK, BLK)


def project_kernel(pos_ref, x_ref, *refs):
    own_ref, first_ref, last_ref, out_ref = refs
    middle = [first_ref[ZN:], last_ref[: ZN // 2]]
    pieces = [own_ref[...], first_ref[:ZN], jnp.concatenate(middle), last_ref[ZN // 2 :]]
    total = jnp.zeros((PAIR, WIDTH), jnp.float32)
    for x_shift in range(XN):
        x_index = lax.rem(pos_ref[1] + XN - x_shift, XN)
        rows = jnp.concatenate(
            [x_ref[:, pl.ds(column_of(pos_ref[0], x_index, shift), BLK)] for shift in range(ZN)],
            axis=1,
        )
        total += dot(rows, pieces[x_shift].reshape(ZN * BLK, WIDTH), ((1,), (0,)))
    out_ref[...] = total.astype(jnp.bfloat16)


def project(position, rows, own, first, last):
    pieces = [
        pl.BlockSpec((count, BLK, WIDTH), lambda i, pos_ref: (0, 0, 0)) for count in (ZN, HALF, HALF)
    ]
    return pl.pallas_call(
        project_kernel,
        grid_spec=pltpu.PrefetchScalarGridSpec(
            num_scalar_prefetch=1,
            grid=(CTX // PAIR,),
            in_specs=[pl.BlockSpec((PAIR, DM), lambda i, pos_ref: (i, 0)), *pieces],
            out_specs=pl.BlockSpec((PAIR, WIDTH), lambda i, pos_ref: (i, 0)),
        ),
        out_shape=jax.ShapeDtypeStruct((CTX, WIDTH), jnp.bfloat16),
        compiler_params=pltpu.CompilerParams(vmem_limit_bytes=16 * MIB),
        cost_estimate=pl.CostEstimate(
            flops=2 * CTX * DM * WIDTH,
            bytes_accessed=2 * (CTX * DM + DM * WIDTH + CTX * WIDTH),
            transcendentals=0,
        ),
        name="project",
    )(position, rows, own, first, last)


def attend_local_kernel(query_ref, local_ref, grad_ref, *out_refs):
    sum_ref, slope_ref, base_ref, stat_ref = out_refs
    row = lax.broadcasted_iota(jnp.int32, (BLK, BLK), 0)
    col = lax.broadcasted_iota(jnp.int32, (BLK, BLK), 1)
    causal = row >= col
    heads = range(HEADS)
    feats = [slice(head * HD, (head + 1) * HD) for head in heads]
    for tile in range(TILES):
        rows = slice(tile * BLK, (tile + 1) * BLK)
        seen = slice(0, (tile + 1) * BLK)
        scores = [dot(query_ref[rows, f], local_ref[0, seen, f], ((1,), (1,))) for f in feats]
        dprobs = [dot(grad_ref[rows, f], local_ref[1, seen, f], ((1,), (1,))) for f in feats]
        last = [jnp.where(causal, s[:, -BLK:] * SCALE, NEG_FILL) for s in scores]
        if tile:
            scores = [
                jnp.concatenate([scores[h][:, :-BLK] * SCALE, last[h]], axis=1) for h in heads
            ]
        else:
            scores = last
        row_max = [jnp.max(s, axis=1, keepdims=True) for s in scores]
        exps = [jnp.exp(scores[h] - row_max[h]) for h in heads]
        total = [jnp.sum(e, axis=1, keepdims=True) for e in exps]
        weights = [e.astype(jnp.bfloat16) for e in exps]
        for h in heads:
            part = dot(weights[h], local_ref[1, seen, feats[h]], ((1,), (0,)))
            sum_ref[rows, feats[h]] = part.astype(jnp.bfloat16)
            part = dot(weights[h], local_ref[0, seen, feats[h]], ((1,), (0,)))
            base_ref[rows, feats[h]] = part.astype(jnp.bfloat16)
        delta = [
            jnp.sum(exps[h] * dprobs[h], axis=1, keepdims=True) / total[h] for h in heads
        ]
        slopes = [(exps[h] * (dprobs[h] - delta[h])).astype(jnp.bfloat16) for h in heads]
        for h in heads:
            part = dot(slopes[h], local_ref[0, seen, feats[h]], ((1,), (0,)))
            slope_ref[rows, feats[h]] = part.astype(jnp.bfloat16)
            for i, stat in enumerate((row_max[h], total[h], delta[h])):
                stat_ref[rows, 3 * h + i : 3 * h + i + 1] = stat


def attend_local(queries, local_kv, grad_out):
    in_vmem = pl.BlockSpec(memory_space=pltpu.VMEM)
    keys_count = BLK * TILES * (TILES + 1) // 2
    return pl.pallas_call(
        attend_local_kernel,
        in_specs=[in_vmem] * 3,
        out_specs=[in_vmem] * 4,
        out_shape=[jax.ShapeDtypeStruct((CTX, WIDTH), jnp.bfloat16)] * 3
        + [jax.ShapeDtypeStruct((CTX, BLK), jnp.float32)],
        compiler_params=pltpu.CompilerParams(vmem_limit_bytes=10 * MIB),
        cost_estimate=pl.CostEstimate(
            flops=10 * BLK * keys_count * WIDTH,
            bytes_accessed=2 * 12 * CTX * WIDTH,
            transcendentals=BLK * keys_count * HEADS,
        ),
        name="attend_local",
    )(queries, local_kv, grad_out)


def attend_memory_kernel(shifts, pos_ref, *refs):
    count, parts = len(shifts), PAIR // BLK
    row_refs, memory_ref, refs = refs[:6], refs[6], refs[7:]
    row_scrs, (held, sems, row_sems), refs = refs[-9:-3], refs[-3:], refs[:-9]
    other_refs, back_refs = refs[:-count], refs[-count:]
    query_scr, grad_scr, sum_scr, slope_scr, base_scr, stat_scr = row_scrs
    groups = [lax.rem(pos_ref[2] + shift, YN) for shift in shifts]
    row_copies = [
        pltpu.make_async_copy(
            ref.at[pl.ds(pl.multiple_of(group * PAIR, PAIR), PAIR)], scr.at[i], row_sems.at[i, j]
        )
        for i, group in enumerate(groups)
        for j, (ref, scr) in enumerate(zip(row_refs, row_scrs))
    ]
    copies = [
        pltpu.make_async_copy(
            memory_ref.at[pos_ref[4 + (group * parts + part) * TOPK + slot]],
            held.at[i * parts + part, slot],
            sems.at[i * parts + part, slot],
        )
        for i, group in enumerate(groups)
        for part in range(parts)
        for slot in range(TOPK)
    ]
    for i in range(count):
        for copy in copies[i * parts * TOPK : (i + 1) * parts * TOPK]:
            copy.start()
        for copy in row_copies[i * 6 : i * 6 + 6]:
            copy.start()
    if shifts == (0,):
        *done_refs, whole_ref = other_refs
        for shift, done_ref in zip(FAR, done_refs):
            group = lax.rem(pos_ref[2] + shift, YN)
            whole_ref[pl.ds(pl.multiple_of(group * PAIR, PAIR), PAIR), :] = done_ref[...]
    for i, group in enumerate(groups):
        for copy in copies[i * parts * TOPK : (i + 1) * parts * TOPK]:
            copy.wait()
        for copy in row_copies[i * 6 : i * 6 + 6]:
            copy.wait()
        units = [(part, head) for part in range(parts) for head in range(HEADS)]
        every = range(len(units))
        rows = [slice(part * BLK, (part + 1) * BLK) for part, head in units]
        feats = [slice(head * HD, (head + 1) * HD) for part, head in units]
        keys, values = [
            [
                held[i * parts + part, :, kind, :, feats[u]].reshape(TOPK * BLK, HD)
                for u, (part, head) in enumerate(units)
            ]
            for kind in range(2)
        ]
        scores = [dot(query_scr[i, rows[u], feats[u]], keys[u], ((1,), (1,))) * SCALE for u in every]
        dprobs = [dot(grad_scr[i, rows[u], feats[u]], values[u], ((1,), (1,))) for u in every]
        stats = [
            [stat_scr[i, rows[u], 3 * head + j : 3 * head + j + 1] for j in range(3)]
            for u, (part, head) in enumerate(units)
        ]
        row_max = [
            jnp.maximum(jnp.max(scores[u], axis=1, keepdims=True), stats[u][0]) for u in every
        ]
        exps = [jnp.exp(scores[u] - row_max[u]) for u in every]
        factor = [jnp.exp(stats[u][0] - row_max[u]) for u in every]
        inverse = [
            1.0 / (jnp.sum(exps[u], axis=1, keepdims=True) + factor[u] * stats[u][1])
            for u in every
        ]
        delta = [
            inverse[u]
            * (
                jnp.sum(exps[u] * dprobs[u], axis=1, keepdims=True)
                + factor[u] * stats[u][1] * stats[u][2]
            )
            for u in every
        ]
        dscores = [(exps[u] * (dprobs[u] - delta[u])).astype(jnp.bfloat16) for u in every]
        for u, (part, head) in enumerate(units):
            back = dot(dscores[u], keys[u], ((1,), (0,))) + factor[u] * (
                slope_scr[i, rows[u], feats[u]].astype(jnp.float32)
                + (stats[u][2] - delta[u]) * base_scr[i, rows[u], feats[u]].astype(jnp.float32)
            )
            back_refs[i][rows[u], feats[u]] = (back * (inverse[u] * SCALE)).astype(jnp.bfloat16)
        for u, (part, head) in enumerate(units):
            attended = factor[u] * sum_scr[i, rows[u], feats[u]].astype(jnp.float32) + dot(
                exps[u].astype(jnp.bfloat16), values[u], ((1,), (0,))
            )
            attended = (attended * inverse[u]).astype(jnp.bfloat16)
            if shifts == (0,):
                whole_ref[pl.ds(pl.multiple_of(group * PAIR + part * BLK, BLK), BLK), feats[u]] = (
                    attended
                )
            else:
                other_refs[i][rows[u], feats[u]] = attended


def attend_memory(shifts, scalars, queries, received, grad_out, prepared, done):
    in_smem, in_vmem = (pl.BlockSpec(memory_space=space) for space in (pltpu.SMEM, pltpu.VMEM))
    count, tiles = len(shifts), len(shifts) * (PAIR // BLK)
    part = jax.ShapeDtypeStruct((PAIR, WIDTH), jnp.bfloat16)
    whole = [jax.ShapeDtypeStruct((CTX, WIDTH), jnp.bfloat16)]
    operands = [queries, grad_out, *prepared, received, *done]
    out_shape = (whole if done else [part] * count) + [part] * count
    keys_count = tiles * TOPK * BLK
    outs = pl.pallas_call(
        functools.partial(attend_memory_kernel, shifts),
        in_specs=[in_smem]
        + [pl.BlockSpec(memory_space=pl.ANY)] * 7
        + [in_vmem] * len(done),
        out_specs=[in_vmem] * len(out_shape),
        out_shape=out_shape,
        scratch_shapes=[pltpu.VMEM((count, PAIR, WIDTH), jnp.bfloat16)] * 5
        + [
            pltpu.VMEM((count, PAIR, BLK), jnp.float32),
            pltpu.VMEM((tiles, TOPK, 2, BLK, WIDTH), jnp.bfloat16),
            pltpu.SemaphoreType.DMA((tiles, TOPK)),
            pltpu.SemaphoreType.DMA((count, 6)),
        ],
        compiler_params=pltpu.CompilerParams(vmem_limit_bytes=58 * MIB),
        cost_estimate=pl.CostEstimate(
            flops=8 * BLK * keys_count * WIDTH,
            bytes_accessed=2 * 12 * CTX * WIDTH,
            transcendentals=BLK * keys_count * HEADS,
        ),
        name="attend_memory",
    )(scalars, *operands)
    return outs[:-count], outs[-count:]


PLACES = (
    (0, 0, ZN),
    (1, 0, ZN),
    (2, 0, ZN),
    (3, 0, ZN),
    *[(shift, ZN + part * HALF, HALF) for shift in range(YN) for part in range(2)],
)


def back_kernel(pos_ref, *refs):
    grad_refs, piece_refs = refs[:YN], refs[YN : YN + len(PLACES)]
    own_ref, send_ref, held, total_scr, sems = refs[YN + len(PLACES) :]
    copies = [
        pltpu.make_async_copy(piece, held.at[shift, pl.ds(first, count)], sems.at[i])
        for i, (piece, (shift, first, count)) in enumerate(zip(piece_refs, PLACES))
    ]
    for copy in copies:
        copy.start()
    core = pos_ref[3]
    own_rows = pl.ds(pl.multiple_of(core * BLK, BLK), BLK)
    send_rows = pl.ds(pl.multiple_of((1 - core) * BLK, BLK), BLK)
    for x_shift in range(XN):
        x_index = lax.rem(pos_ref[1] + XN - x_shift, XN)
        if x_shift < 2:
            for copy in copies[YN:] if x_shift else copies[:YN]:
                copy.wait()
        blocks = slice(x_shift * ZN, (x_shift + 1) * ZN)
        total = jnp.zeros((PAIR, ZN * BLK), jnp.float32)
        for shift in range(YN):
            weight = held[shift, blocks].reshape(ZN * BLK, WIDTH)
            total += dot(grad_refs[shift][...], weight, ((1,), (1,)))
        total_scr[...] = total
        for out_ref, rows in ((send_ref, send_rows), (own_ref, own_rows)):
            for shift in range(ZN):
                columns = pl.ds(column_of(pos_ref[0], x_index, shift), BLK)
                part = total_scr[rows, shift * BLK : (shift + 1) * BLK]
                out_ref[:, columns] = part.astype(out_ref.dtype)


def back_project(position, grads, pieces):
    in_vmem = pl.BlockSpec(memory_space=pltpu.VMEM)
    return pl.pallas_call(
        back_kernel,
        in_specs=[pl.BlockSpec(memory_space=pltpu.SMEM)]
        + [in_vmem] * YN
        + [pl.BlockSpec(memory_space=pl.ANY)] * len(pieces),
        out_specs=[in_vmem] * 2,
        out_shape=[
            jax.ShapeDtypeStruct((BLK, DM), jnp.float32),
            jax.ShapeDtypeStruct((BLK, DM), jnp.bfloat16),
        ],
        scratch_shapes=[
            pltpu.VMEM((YN, XN * ZN, BLK, WIDTH), jnp.bfloat16),
            pltpu.VMEM((PAIR, ZN * BLK), jnp.float32),
            pltpu.SemaphoreType.DMA((len(pieces),)),
        ],
        compiler_params=pltpu.CompilerParams(vmem_limit_bytes=20 * MIB),
        cost_estimate=pl.CostEstimate(
            flops=2 * PAIR * DM * YN * WIDTH,
            bytes_accessed=2 * (2 * PAIR * DM + DM * YN * WIDTH),
            transcendentals=0,
        ),
        name="back_project",
    )(position, *grads, *pieces)


def move(array, axis, count, shift):
    if shift % count == 0:
        return array
    return lax.ppermute(array, axis, [(i, (i + shift) % count) for i in range(count)])


def local(layer_input, w_query, local_kv, memory_kv, memory_ids, grad_out):
    position = jnp.stack([lax.axis_index(axis) for axis in ("z", "x", "y", "c")]).astype(jnp.int32)
    owner_of = memory_ids // MB_DEV
    scalars = jnp.concatenate([position, owner_of.reshape(TILES * TOPK)])
    owners = jnp.arange(OWNERS, dtype=jnp.int32)
    wanted = jnp.max(
        jnp.where(owner_of[:, :, None] == owners, (memory_ids % MB_DEV)[:, :, None], 0),
        axis=(0, 1),
    )
    weights = [move(w_query, "z", ZN, shift) for shift in range(ZN)]
    asked = lax.all_to_all(wanted.reshape(OWNERS, 1), MEM, 0, 0, tiled=True)
    asked, weights = lax.optimization_barrier((asked, weights))
    received = lax.all_to_all(pick_blocks(asked[:, 0], memory_kv), MEM, 0, 0, tiled=True)
    own = jnp.stack(weights)
    rows = lax.all_gather(layer_input, ("y", "c"), axis=0, tiled=True)
    others = [move(own, "x", XN, shift) for shift in range(1, XN)]
    first = jnp.concatenate([others[0], others[1][: ZN // 2]])
    last = jnp.concatenate([others[1][ZN // 2 :], others[2]])
    near_parts = [own, *[move(own, "y", YN, shift) for shift in range(1, YN)]]
    first, last, near_parts = lax.optimization_barrier((first, last, near_parts))
    below, above = move(first, "y", YN, 1), move(last, "y", YN, -1)
    below_last, above_first = move(last, "y", YN, 1), move(first, "y", YN, -1)
    queries = project(scalars, rows, own, first, last)
    *sums, stats = attend_local(queries, local_kv, grad_out)
    below, above, stats = lax.optimization_barrier((below, above, stats))
    prepared = [*sums, stats]
    far_first, far_last = move(below, "y", YN, 1), move(above, "y", YN, -1)
    rest = [first, last, below, below_last, far_first, far_last, above_first, above]
    pieces = [*near_parts, *rest]
    done, far = attend_memory(FAR, scalars, queries, received, grad_out, prepared, [])
    far = {shift: move(part, "y", YN, shift) for shift, part in zip(FAR, far)}
    (attended,), (near,) = attend_memory(
        (0,), scalars, queries, received, grad_out, prepared, done
    )
    grads = [near, far[1], far[2], far[3]]
    own_part, send = back_project(scalars, grads, pieces)
    other = move(send, "c", CN, 1)
    return (attended, (own_part + other.astype(jnp.float32)).astype(jnp.bfloat16))


def solution(mesh):
    torus = Mesh(mesh.devices.reshape(ZN, XN, YN, CN), ("z", "x", "y", "c"))
    in_specs = (
        P(("z", "x", "y", "c"), None),
        P(MEM, ("y", "c")),
        P(None, MEM, ("y", "c")),
        P(MEM, None, None, ("y", "c")),
        P(MEM, None),
        P(MEM, ("y", "c")),
    )
    out_specs = (P(MEM, ("y", "c")), P(("z", "x", "y", "c"), None))
    return jax.shard_map(local, mesh=torus, in_specs=in_specs, out_specs=out_specs, check_vma=False)
```

```python
import functools
import functools
import math

import jax
import jax.numpy as jnp
from jax import lax
from jax.experimental import pallas as pl
from jax.experimental.pallas import tpu as pltpu
from jax.sharding import Mesh
from jax.sharding import PartitionSpec as P

HD = 128
BLK = 128
TOPK = 4
MB_DEV = 16
CTX = 1024
TILES = CTX // BLK
ZN, XN, YN, CN = 8, 4, 4, 2
OWNERS = ZN * XN
HEADS = 2
WIDTH = HEADS * HD
DM = 4096
PAIR = 2 * BLK
MEM = ("z", "x")
MIB = 1024 * 1024
PICK_PARTS = 4
Z_ORDER = (0, 4, 1, 5, 2, 6, 7, 3)
HALF = (XN - 1) * ZN // 2
NEG_FILL = -1e30
SCALE = 1.0 / math.sqrt(HD)
FAR = (2, 1, 3)


def dot(a, b, dims):
    return lax.dot_general(a, b, (dims, ((), ())), preferred_element_type=jnp.float32)


def pick_kernel(asked_ref, memory_ref, out_ref, held, in_sems, out_sems):
    count = MB_DEV // PICK_PARTS
    loads = [
        pltpu.make_async_copy(
            memory_ref.at[pl.ds(i * count, count)], held.at[pl.ds(i * count, count)], in_sems.at[i]
        )
        for i in range(PICK_PARTS)
    ]
    stores = [
        pltpu.make_async_copy(held.at[asked_ref[i]], out_ref.at[i], out_sems.at[i])
        for i in range(OWNERS)
    ]
    for copies in (loads, stores):
        for copy in copies:
            copy.start()
        for copy in copies:
            copy.wait()


def pick_blocks(asked, memory_kv):
    anywhere = pl.BlockSpec(memory_space=pl.ANY)
    return pl.pallas_call(
        pick_kernel,
        in_specs=[pl.BlockSpec(memory_space=pltpu.SMEM), anywhere],
        out_specs=anywhere,
        out_shape=jax.ShapeDtypeStruct((OWNERS, 2, BLK, WIDTH), jnp.bfloat16),
        scratch_shapes=[
            pltpu.VMEM((MB_DEV, 2, BLK, WIDTH), jnp.bfloat16),
            pltpu.SemaphoreType.DMA((PICK_PARTS,)),
            pltpu.SemaphoreType.DMA((OWNERS,)),
        ],
        compiler_params=pltpu.CompilerParams(vmem_limit_bytes=58 * MIB),
        cost_estimate=pl.CostEstimate(
            flops=0, bytes_accessed=2 * OWNERS * 2 * BLK * WIDTH * 2, transcendentals=0
        ),
        name="pick_blocks",
    )(asked, memory_kv)


def column_of(z_index, x_index, shift):
    return pl.multiple_of((lax.rem(z_index + ZN - shift, ZN) * XN + x_index) * BLK, BLK)


def project_kernel(pos_ref, x_ref, *refs):
    own_ref, first_ref, last_ref, out_ref = refs
    middle = [first_ref[ZN:], last_ref[: ZN // 2]]
    pieces = [own_ref[...], first_ref[:ZN], jnp.concatenate(middle), last_ref[ZN // 2 :]]
    total = jnp.zeros((PAIR, WIDTH), jnp.float32)
    for x_shift in range(XN):
        x_index = lax.rem(pos_ref[1] + XN - x_shift, XN)
        rows = jnp.concatenate(
            [x_ref[:, pl.ds(column_of(pos_ref[0], x_index, shift), BLK)] for shift in Z_ORDER],
            axis=1,
        )
        total += dot(rows, pieces[x_shift].reshape(ZN * BLK, WIDTH), ((1,), (0,)))
    out_ref[...] = total.astype(jnp.bfloat16)


def project(position, rows, own, first, last):
    pieces = [
        pl.BlockSpec((count, BLK, WIDTH), lambda i, pos_ref: (0, 0, 0)) for count in (ZN, HALF, HALF)
    ]
    return pl.pallas_call(
        project_kernel,
        grid_spec=pltpu.PrefetchScalarGridSpec(
            num_scalar_prefetch=1,
            grid=(CTX // PAIR,),
            in_specs=[pl.BlockSpec((PAIR, DM), lambda i, pos_ref: (i, 0)), *pieces],
            out_specs=pl.BlockSpec((PAIR, WIDTH), lambda i, pos_ref: (i, 0)),
        ),
        out_shape=jax.ShapeDtypeStruct((CTX, WIDTH), jnp.bfloat16),
        compiler_params=pltpu.CompilerParams(vmem_limit_bytes=16 * MIB),
        cost_estimate=pl.CostEstimate(
            flops=2 * CTX * DM * WIDTH,
            bytes_accessed=2 * (CTX * DM + DM * WIDTH + CTX * WIDTH),
            transcendentals=0,
        ),
        name="project",
    )(position, rows, own, first, last)


def attend_local_kernel(query_ref, local_ref, grad_ref, *out_refs):
    sum_ref, slope_ref, base_ref, stat_ref = out_refs
    row = lax.broadcasted_iota(jnp.int32, (BLK, BLK), 0)
    col = lax.broadcasted_iota(jnp.int32, (BLK, BLK), 1)
    causal = row >= col
    heads = range(HEADS)
    feats = [slice(head * HD, (head + 1) * HD) for head in heads]
    for tile in range(TILES):
        rows = slice(tile * BLK, (tile + 1) * BLK)
        seen = slice(0, (tile + 1) * BLK)
        scores = [dot(query_ref[rows, f], local_ref[0, seen, f], ((1,), (1,))) for f in feats]
        dprobs = [dot(grad_ref[rows, f], local_ref[1, seen, f], ((1,), (1,))) for f in feats]
        last = [jnp.where(causal, s[:, -BLK:] * SCALE, NEG_FILL) for s in scores]
        if tile:
            scores = [
                jnp.concatenate([scores[h][:, :-BLK] * SCALE, last[h]], axis=1) for h in heads
            ]
        else:
            scores = last
        row_max = [jnp.max(s, axis=1, keepdims=True) for s in scores]
        exps = [jnp.exp(scores[h] - row_max[h]) for h in heads]
        total = [jnp.sum(e, axis=1, keepdims=True) for e in exps]
        weights = [e.astype(jnp.bfloat16) for e in exps]
        for h in heads:
            part = dot(weights[h], local_ref[1, seen, feats[h]], ((1,), (0,)))
            sum_ref[rows, feats[h]] = part.astype(jnp.bfloat16)
            part = dot(weights[h], local_ref[0, seen, feats[h]], ((1,), (0,)))
            base_ref[rows, feats[h]] = part.astype(jnp.bfloat16)
        delta = [
            jnp.sum(exps[h] * dprobs[h], axis=1, keepdims=True) / total[h] for h in heads
        ]
        slopes = [(exps[h] * (dprobs[h] - delta[h])).astype(jnp.bfloat16) for h in heads]
        for h in heads:
            part = dot(slopes[h], local_ref[0, seen, feats[h]], ((1,), (0,)))
            slope_ref[rows, feats[h]] = part.astype(jnp.bfloat16)
            for i, stat in enumerate((row_max[h], total[h], delta[h])):
                stat_ref[rows, 3 * h + i : 3 * h + i + 1] = stat


def attend_local(queries, local_kv, grad_out):
    in_vmem = pl.BlockSpec(memory_space=pltpu.VMEM)
    keys_count = BLK * TILES * (TILES + 1) // 2
    return pl.pallas_call(
        attend_local_kernel,
        in_specs=[in_vmem] * 3,
        out_specs=[in_vmem] * 4,
        out_shape=[jax.ShapeDtypeStruct((CTX, WIDTH), jnp.bfloat16)] * 3
        + [jax.ShapeDtypeStruct((CTX, BLK), jnp.float32)],
        compiler_params=pltpu.CompilerParams(vmem_limit_bytes=10 * MIB),
        cost_estimate=pl.CostEstimate(
            flops=10 * BLK * keys_count * WIDTH,
            bytes_accessed=2 * 12 * CTX * WIDTH,
            transcendentals=BLK * keys_count * HEADS,
        ),
        name="attend_local",
    )(queries, local_kv, grad_out)


def attend_memory_kernel(shifts, pos_ref, *refs):
    count, parts = len(shifts), PAIR // BLK
    row_refs, memory_ref, refs = refs[:6], refs[6], refs[7:]
    row_scrs, (held, sems, row_sems), refs = refs[-9:-3], refs[-3:], refs[:-9]
    other_refs, back_refs = refs[:-count], refs[-count:]
    query_scr, grad_scr, sum_scr, slope_scr, base_scr, stat_scr = row_scrs
    groups = [lax.rem(pos_ref[2] + shift, YN) for shift in shifts]
    row_copies = [
        pltpu.make_async_copy(
            ref.at[pl.ds(pl.multiple_of(group * PAIR, PAIR), PAIR)], scr.at[i], row_sems.at[i, j]
        )
        for i, group in enumerate(groups)
        for j, (ref, scr) in enumerate(zip(row_refs, row_scrs))
    ]
    copies = [
        pltpu.make_async_copy(
            memory_ref.at[pos_ref[4 + (group * parts + part) * TOPK + slot]],
            held.at[i * parts + part, slot],
            sems.at[i * parts + part, slot],
        )
        for i, group in enumerate(groups)
        for part in range(parts)
        for slot in range(TOPK)
    ]
    grouped = [
        copies[i * parts * TOPK : (i + 1) * parts * TOPK] + row_copies[i * 6 : i * 6 + 6]
        for i in range(count)
    ]
    for copy in grouped[0]:
        copy.start()
    if shifts == (0,):
        *done_refs, whole_ref = other_refs
        for shift, done_ref in zip(FAR, done_refs):
            group = lax.rem(pos_ref[2] + shift, YN)
            whole_ref[pl.ds(pl.multiple_of(group * PAIR, PAIR), PAIR), :] = done_ref[...]
    for i, group in enumerate(groups):
        for copy in grouped[i]:
            copy.wait()
        for copy in grouped[i + 1] if i + 1 < count else []:
            copy.start()
        units = [(part, head) for part in range(parts) for head in range(HEADS)]
        every = range(len(units))
        rows = [slice(part * BLK, (part + 1) * BLK) for part, head in units]
        feats = [slice(head * HD, (head + 1) * HD) for part, head in units]
        keys, values = [
            [
                held[i * parts + part, :, kind, :, feats[u]].reshape(TOPK * BLK, HD)
                for u, (part, head) in enumerate(units)
            ]
            for kind in range(2)
        ]
        scores = [dot(query_scr[i, rows[u], feats[u]], keys[u], ((1,), (1,))) * SCALE for u in every]
        dprobs = [dot(grad_scr[i, rows[u], feats[u]], values[u], ((1,), (1,))) for u in every]
        stats = [
            [stat_scr[i, rows[u], 3 * head + j : 3 * head + j + 1] for j in range(3)]
            for u, (part, head) in enumerate(units)
        ]
        row_max = [
            jnp.maximum(jnp.max(scores[u], axis=1, keepdims=True), stats[u][0]) for u in every
        ]
        exps = [jnp.exp(scores[u] - row_max[u]) for u in every]
        factor = [jnp.exp(stats[u][0] - row_max[u]) for u in every]
        inverse = [
            1.0 / (jnp.sum(exps[u], axis=1, keepdims=True) + factor[u] * stats[u][1])
            for u in every
        ]
        delta = [
            inverse[u]
            * (
                jnp.sum(exps[u] * dprobs[u], axis=1, keepdims=True)
                + factor[u] * stats[u][1] * stats[u][2]
            )
            for u in every
        ]
        dscores = [(exps[u] * (dprobs[u] - delta[u])).astype(jnp.bfloat16) for u in every]
        for u, (part, head) in enumerate(units):
            back = dot(dscores[u], keys[u], ((1,), (0,))) + factor[u] * (
                slope_scr[i, rows[u], feats[u]].astype(jnp.float32)
                + (stats[u][2] - delta[u]) * base_scr[i, rows[u], feats[u]].astype(jnp.float32)
            )
            back_refs[i][rows[u], feats[u]] = (back * (inverse[u] * SCALE)).astype(jnp.bfloat16)
        for u, (part, head) in enumerate(units):
            attended = factor[u] * sum_scr[i, rows[u], feats[u]].astype(jnp.float32) + dot(
                exps[u].astype(jnp.bfloat16), values[u], ((1,), (0,))
            )
            attended = (attended * inverse[u]).astype(jnp.bfloat16)
            if shifts == (0,):
                whole_ref[pl.ds(pl.multiple_of(group * PAIR + part * BLK, BLK), BLK), feats[u]] = (
                    attended
                )
            else:
                other_refs[i][rows[u], feats[u]] = attended


def attend_memory(shifts, scalars, queries, received, grad_out, prepared, done):
    in_smem, in_vmem = (pl.BlockSpec(memory_space=space) for space in (pltpu.SMEM, pltpu.VMEM))
    count, tiles = len(shifts), len(shifts) * (PAIR // BLK)
    part = jax.ShapeDtypeStruct((PAIR, WIDTH), jnp.bfloat16)
    whole = [jax.ShapeDtypeStruct((CTX, WIDTH), jnp.bfloat16)]
    operands = [queries, grad_out, *prepared, received, *done]
    out_shape = (whole if done else [part] * count) + [part] * count
    keys_count = tiles * TOPK * BLK
    outs = pl.pallas_call(
        functools.partial(attend_memory_kernel, shifts),
        in_specs=[in_smem]
        + [pl.BlockSpec(memory_space=pl.ANY)] * 7
        + [in_vmem] * len(done),
        out_specs=[in_vmem] * len(out_shape),
        out_shape=out_shape,
        scratch_shapes=[pltpu.VMEM((count, PAIR, WIDTH), jnp.bfloat16)] * 5
        + [
            pltpu.VMEM((count, PAIR, BLK), jnp.float32),
            pltpu.VMEM((tiles, TOPK, 2, BLK, WIDTH), jnp.bfloat16),
            pltpu.SemaphoreType.DMA((tiles, TOPK)),
            pltpu.SemaphoreType.DMA((count, 6)),
        ],
        compiler_params=pltpu.CompilerParams(vmem_limit_bytes=58 * MIB),
        cost_estimate=pl.CostEstimate(
            flops=8 * BLK * keys_count * WIDTH,
            bytes_accessed=2 * 12 * CTX * WIDTH,
            transcendentals=BLK * keys_count * HEADS,
        ),
        name="attend_memory",
    )(scalars, *operands)
    return outs[:-count], outs[-count:]


PLACES = (
    (0, 0, ZN),
    (1, 0, ZN),
    (2, 0, ZN),
    (3, 0, ZN),
    *[(shift, ZN + part * HALF, HALF) for shift in range(YN) for part in range(2)],
)


def back_kernel(pos_ref, *refs):
    grad_refs, piece_refs = refs[:YN], refs[YN : YN + len(PLACES)]
    own_ref, send_ref, held, total_scr, sems = refs[YN + len(PLACES) :]
    copies = [
        pltpu.make_async_copy(piece, held.at[shift, pl.ds(first, count)], sems.at[i])
        for i, (piece, (shift, first, count)) in enumerate(zip(piece_refs, PLACES))
    ]
    stages = [copies[:YN], copies[YN::2], copies[YN + 1 :: 2]]
    for copy in stages[0] + stages[1]:
        copy.start()
    core = pos_ref[3]
    own_rows = pl.ds(pl.multiple_of(core * BLK, BLK), BLK)
    send_rows = pl.ds(pl.multiple_of((1 - core) * BLK, BLK), BLK)
    for x_shift in range(XN):
        x_index = lax.rem(pos_ref[1] + XN - x_shift, XN)
        for copy in stages[x_shift] if x_shift < len(stages) else []:
            copy.wait()
        for copy in stages[2] if x_shift == 0 else []:
            copy.start()
        blocks = slice(x_shift * ZN, (x_shift + 1) * ZN)
        total = jnp.zeros((PAIR, ZN * BLK), jnp.float32)
        for shift in range(YN):
            weight = held[shift, blocks].reshape(ZN * BLK, WIDTH)
            total += dot(grad_refs[shift][...], weight, ((1,), (1,)))
        total_scr[...] = total
        for out_ref, rows in ((send_ref, send_rows), (own_ref, own_rows)):
            for i, shift in enumerate(Z_ORDER):
                columns = pl.ds(column_of(pos_ref[0], x_index, shift), BLK)
                part = total_scr[rows, i * BLK : (i + 1) * BLK]
                out_ref[:, columns] = part.astype(out_ref.dtype)


def back_project(position, grads, pieces):
    in_vmem = pl.BlockSpec(memory_space=pltpu.VMEM)
    return pl.pallas_call(
        back_kernel,
        in_specs=[pl.BlockSpec(memory_space=pltpu.SMEM)]
        + [in_vmem] * YN
        + [pl.BlockSpec(memory_space=pl.ANY)] * len(pieces),
        out_specs=[in_vmem] * 2,
        out_shape=[
            jax.ShapeDtypeStruct((BLK, DM), jnp.float32),
            jax.ShapeDtypeStruct((BLK, DM), jnp.bfloat16),
        ],
        scratch_shapes=[
            pltpu.VMEM((YN, XN * ZN, BLK, WIDTH), jnp.bfloat16),
            pltpu.VMEM((PAIR, ZN * BLK), jnp.float32),
            pltpu.SemaphoreType.DMA((len(pieces),)),
        ],
        compiler_params=pltpu.CompilerParams(vmem_limit_bytes=20 * MIB),
        cost_estimate=pl.CostEstimate(
            flops=2 * PAIR * DM * YN * WIDTH,
            bytes_accessed=2 * (2 * PAIR * DM + DM * YN * WIDTH),
            transcendentals=0,
        ),
        name="back_project",
    )(position, *grads, *pieces)


def move(array, axis, count, shift):
    if shift % count == 0:
        return array
    return lax.ppermute(array, axis, [(i, (i + shift) % count) for i in range(count)])


def local(layer_input, w_query, local_kv, memory_kv, memory_ids, grad_out):
    position = jnp.stack([lax.axis_index(axis) for axis in ("z", "x", "y", "c")]).astype(jnp.int32)
    owner_of = memory_ids // MB_DEV
    scalars = jnp.concatenate([position, owner_of.reshape(TILES * TOPK)])
    owners = jnp.arange(OWNERS, dtype=jnp.int32)
    wanted = jnp.max(
        jnp.where(owner_of[:, :, None] == owners, (memory_ids % MB_DEV)[:, :, None], 0),
        axis=(0, 1),
    )
    pair = jnp.stack([w_query, move(w_query, "z", ZN, 4)])
    weights = [pair, *[move(pair, "z", ZN, shift) for shift in (1, 2, -1)]]
    asked = lax.all_to_all(wanted.reshape(OWNERS, 1), MEM, 0, 0, tiled=True)
    asked, weights = lax.optimization_barrier((asked, weights))
    received = lax.all_to_all(pick_blocks(asked[:, 0], memory_kv), MEM, 0, 0, tiled=True)
    own = jnp.concatenate(weights)
    rows = lax.all_gather(layer_input, ("y", "c"), axis=0, tiled=True)
    others = [move(own, "x", XN, shift) for shift in range(1, XN)]
    first = jnp.concatenate([others[0], others[1][: ZN // 2]])
    last = jnp.concatenate([others[1][ZN // 2 :], others[2]])
    near_parts = [own, *[move(own, "y", YN, shift) for shift in range(1, YN)]]
    first, last, near_parts = lax.optimization_barrier((first, last, near_parts))
    below, above = move(first, "y", YN, 1), move(last, "y", YN, -1)
    below_last, above_first = move(last, "y", YN, 1), move(first, "y", YN, -1)
    queries = project(scalars, rows, own, first, last)
    *sums, stats = attend_local(queries, local_kv, grad_out)
    below, above, stats = lax.optimization_barrier((below, above, stats))
    prepared = [*sums, stats]
    far_first, far_last = move(below, "y", YN, 1), move(above, "y", YN, -1)
    rest = [first, last, below, below_last, far_first, far_last, above_first, above]
    pieces = [*near_parts, *rest]
    done, far = attend_memory(FAR, scalars, queries, received, grad_out, prepared, [])
    far = {shift: move(part, "y", YN, shift) for shift, part in zip(FAR, far)}
    (attended,), (near,) = attend_memory(
        (0,), scalars, queries, received, grad_out, prepared, done
    )
    grads = [near, far[1], far[2], far[3]]
    own_part, send = back_project(scalars, grads, pieces)
    other = move(send, "c", CN, 1)
    return (attended, (own_part + other.astype(jnp.float32)).astype(jnp.bfloat16))


def solution(mesh):
    torus = Mesh(mesh.devices.reshape(ZN, XN, YN, CN), ("z", "x", "y", "c"))
    in_specs = (
        P(("z", "x", "y", "c"), None),
        P(MEM, ("y", "c")),
        P(None, MEM, ("y", "c")),
        P(MEM, None, None, ("y", "c")),
        P(MEM, None),
        P(MEM, ("y", "c")),
    )
    out_specs = (P(MEM, ("y", "c")), P(("z", "x", "y", "c"), None))
    return jax.shard_map(local, mesh=torus, in_specs=in_specs, out_specs=out_specs, check_vma=False)
```

```python
import functools
import functools
import math

import jax
import jax.numpy as jnp
from jax import lax
from jax.experimental import pallas as pl
from jax.experimental.pallas import tpu as pltpu
from jax.sharding import Mesh
from jax.sharding import PartitionSpec as P

HD = 128
BLK = 128
TOPK = 4
MB_DEV = 16
CTX = 1024
TILES = CTX // BLK
ZN, XN, YN, CN = 8, 4, 4, 2
OWNERS = ZN * XN
HEADS = 2
WIDTH = HEADS * HD
DM = 4096
PAIR = 2 * BLK
MEM = ("z", "x")
MIB = 1024 * 1024
PICK_PARTS = 4
Z_ORDER = tuple(range(ZN))
HALF = (XN - 1) * ZN // 2
NEG_FILL = -1e30
SCALE = 1.0 / math.sqrt(HD)
FAR = (2, 1, 3)


def dot(a, b, dims):
    return lax.dot_general(a, b, (dims, ((), ())), preferred_element_type=jnp.float32)


def pick_kernel(asked_ref, memory_ref, out_ref, held, in_sems, out_sems):
    count = MB_DEV // PICK_PARTS
    loads = [
        pltpu.make_async_copy(
            memory_ref.at[pl.ds(i * count, count)], held.at[pl.ds(i * count, count)], in_sems.at[i]
        )
        for i in range(PICK_PARTS)
    ]
    stores = [
        pltpu.make_async_copy(held.at[asked_ref[i]], out_ref.at[i], out_sems.at[i])
        for i in range(OWNERS)
    ]
    for copies in (loads, stores):
        for copy in copies:
            copy.start()
        for copy in copies:
            copy.wait()


def pick_blocks(asked, memory_kv):
    anywhere = pl.BlockSpec(memory_space=pl.ANY)
    return pl.pallas_call(
        pick_kernel,
        in_specs=[pl.BlockSpec(memory_space=pltpu.SMEM), anywhere],
        out_specs=anywhere,
        out_shape=jax.ShapeDtypeStruct((OWNERS, 2, BLK, WIDTH), jnp.bfloat16),
        scratch_shapes=[
            pltpu.VMEM((MB_DEV, 2, BLK, WIDTH), jnp.bfloat16),
            pltpu.SemaphoreType.DMA((PICK_PARTS,)),
            pltpu.SemaphoreType.DMA((OWNERS,)),
        ],
        compiler_params=pltpu.CompilerParams(vmem_limit_bytes=58 * MIB),
        cost_estimate=pl.CostEstimate(
            flops=0, bytes_accessed=2 * OWNERS * 2 * BLK * WIDTH * 2, transcendentals=0
        ),
        name="pick_blocks",
    )(asked, memory_kv)


def column_of(z_index, x_index, shift):
    return pl.multiple_of((lax.rem(z_index + ZN - shift, ZN) * XN + x_index) * BLK, BLK)


def project_kernel(pos_ref, x_ref, *refs):
    own_ref, first_ref, last_ref, out_ref = refs
    middle = [first_ref[ZN:], last_ref[: ZN // 2]]
    pieces = [own_ref[...], first_ref[:ZN], jnp.concatenate(middle), last_ref[ZN // 2 :]]
    total = jnp.zeros((PAIR, WIDTH), jnp.float32)
    for x_shift in range(XN):
        x_index = lax.rem(pos_ref[1] + XN - x_shift, XN)
        rows = jnp.concatenate(
            [x_ref[:, pl.ds(column_of(pos_ref[0], x_index, shift), BLK)] for shift in Z_ORDER],
            axis=1,
        )
        total += dot(rows, pieces[x_shift].reshape(ZN * BLK, WIDTH), ((1,), (0,)))
    out_ref[...] = total.astype(jnp.bfloat16)


def project(position, rows, own, first, last):
    pieces = [
        pl.BlockSpec((count, BLK, WIDTH), lambda i, pos_ref: (0, 0, 0)) for count in (ZN, HALF, HALF)
    ]
    return pl.pallas_call(
        project_kernel,
        grid_spec=pltpu.PrefetchScalarGridSpec(
            num_scalar_prefetch=1,
            grid=(CTX // PAIR,),
            in_specs=[pl.BlockSpec((PAIR, DM), lambda i, pos_ref: (i, 0)), *pieces],
            out_specs=pl.BlockSpec((PAIR, WIDTH), lambda i, pos_ref: (i, 0)),
        ),
        out_shape=jax.ShapeDtypeStruct((CTX, WIDTH), jnp.bfloat16),
        compiler_params=pltpu.CompilerParams(vmem_limit_bytes=16 * MIB),
        cost_estimate=pl.CostEstimate(
            flops=2 * CTX * DM * WIDTH,
            bytes_accessed=2 * (CTX * DM + DM * WIDTH + CTX * WIDTH),
            transcendentals=0,
        ),
        name="project",
    )(position, rows, own, first, last)


def attend_local_kernel(query_ref, local_ref, grad_ref, *out_refs):
    sum_ref, slope_ref, base_ref, stat_ref = out_refs
    row = lax.broadcasted_iota(jnp.int32, (BLK, BLK), 0)
    col = lax.broadcasted_iota(jnp.int32, (BLK, BLK), 1)
    causal = row >= col
    heads = range(HEADS)
    feats = [slice(head * HD, (head + 1) * HD) for head in heads]
    for tile in range(TILES):
        rows = slice(tile * BLK, (tile + 1) * BLK)
        seen = slice(0, (tile + 1) * BLK)
        scores = [dot(query_ref[rows, f], local_ref[0, seen, f], ((1,), (1,))) for f in feats]
        dprobs = [dot(grad_ref[rows, f], local_ref[1, seen, f], ((1,), (1,))) for f in feats]
        last = [jnp.where(causal, s[:, -BLK:] * SCALE, NEG_FILL) for s in scores]
        if tile:
            scores = [
                jnp.concatenate([scores[h][:, :-BLK] * SCALE, last[h]], axis=1) for h in heads
            ]
        else:
            scores = last
        row_max = [jnp.max(s, axis=1, keepdims=True) for s in scores]
        exps = [jnp.exp(scores[h] - row_max[h]) for h in heads]
        total = [jnp.sum(e, axis=1, keepdims=True) for e in exps]
        weights = [e.astype(jnp.bfloat16) for e in exps]
        for h in heads:
            part = dot(weights[h], local_ref[1, seen, feats[h]], ((1,), (0,)))
            sum_ref[rows, feats[h]] = part.astype(jnp.bfloat16)
            part = dot(weights[h], local_ref[0, seen, feats[h]], ((1,), (0,)))
            base_ref[rows, feats[h]] = part.astype(jnp.bfloat16)
        delta = [
            jnp.sum(exps[h] * dprobs[h], axis=1, keepdims=True) / total[h] for h in heads
        ]
        slopes = [(exps[h] * (dprobs[h] - delta[h])).astype(jnp.bfloat16) for h in heads]
        for h in heads:
            part = dot(slopes[h], local_ref[0, seen, feats[h]], ((1,), (0,)))
            slope_ref[rows, feats[h]] = part.astype(jnp.bfloat16)
            for i, stat in enumerate((row_max[h], total[h], delta[h])):
                stat_ref[rows, 3 * h + i : 3 * h + i + 1] = stat


def attend_local(queries, local_kv, grad_out):
    in_vmem = pl.BlockSpec(memory_space=pltpu.VMEM)
    keys_count = BLK * TILES * (TILES + 1) // 2
    return pl.pallas_call(
        attend_local_kernel,
        in_specs=[in_vmem] * 3,
        out_specs=[in_vmem] * 4,
        out_shape=[jax.ShapeDtypeStruct((CTX, WIDTH), jnp.bfloat16)] * 3
        + [jax.ShapeDtypeStruct((CTX, BLK), jnp.float32)],
        compiler_params=pltpu.CompilerParams(vmem_limit_bytes=10 * MIB),
        cost_estimate=pl.CostEstimate(
            flops=10 * BLK * keys_count * WIDTH,
            bytes_accessed=2 * 12 * CTX * WIDTH,
            transcendentals=BLK * keys_count * HEADS,
        ),
        name="attend_local",
    )(queries, local_kv, grad_out)


def attend_memory_kernel(shifts, pos_ref, *refs):
    count, parts = len(shifts), PAIR // BLK
    row_refs, memory_ref, refs = refs[:6], refs[6], refs[7:]
    row_scrs, (held, sems, row_sems), refs = refs[-9:-3], refs[-3:], refs[:-9]
    other_refs, back_refs = refs[:-count], refs[-count:]
    query_scr, grad_scr, sum_scr, slope_scr, base_scr, stat_scr = row_scrs
    groups = [lax.rem(pos_ref[2] + shift, YN) for shift in shifts]
    row_copies = [
        pltpu.make_async_copy(
            ref.at[pl.ds(pl.multiple_of(group * PAIR, PAIR), PAIR)], scr.at[i], row_sems.at[i, j]
        )
        for i, group in enumerate(groups)
        for j, (ref, scr) in enumerate(zip(row_refs, row_scrs))
    ]
    copies = [
        pltpu.make_async_copy(
            memory_ref.at[pos_ref[4 + (group * parts + part) * TOPK + slot]],
            held.at[i * parts + part, slot],
            sems.at[i * parts + part, slot],
        )
        for i, group in enumerate(groups)
        for part in range(parts)
        for slot in range(TOPK)
    ]
    grouped = [
        copies[i * parts * TOPK : (i + 1) * parts * TOPK] + row_copies[i * 6 : i * 6 + 6]
        for i in range(count)
    ]
    for copy in grouped[0]:
        copy.start()
    if shifts == (0,):
        *done_refs, whole_ref = other_refs
        for shift, done_ref in zip(FAR, done_refs):
            group = lax.rem(pos_ref[2] + shift, YN)
            whole_ref[pl.ds(pl.multiple_of(group * PAIR, PAIR), PAIR), :] = done_ref[...]
    for i, group in enumerate(groups):
        for copy in grouped[i]:
            copy.wait()
        for copy in grouped[i + 1] if i + 1 < count else []:
            copy.start()
        units = [(part, head) for part in range(parts) for head in range(HEADS)]
        every = range(len(units))
        rows = [slice(part * BLK, (part + 1) * BLK) for part, head in units]
        feats = [slice(head * HD, (head + 1) * HD) for part, head in units]
        keys, values = [
            [
                held[i * parts + part, :, kind, :, feats[u]].reshape(TOPK * BLK, HD)
                for u, (part, head) in enumerate(units)
            ]
            for kind in range(2)
        ]
        scores = [dot(query_scr[i, rows[u], feats[u]], keys[u], ((1,), (1,))) * SCALE for u in every]
        dprobs = [dot(grad_scr[i, rows[u], feats[u]], values[u], ((1,), (1,))) for u in every]
        stats = [
            [stat_scr[i, rows[u], 3 * head + j : 3 * head + j + 1] for j in range(3)]
            for u, (part, head) in enumerate(units)
        ]
        row_max = [
            jnp.maximum(jnp.max(scores[u], axis=1, keepdims=True), stats[u][0]) for u in every
        ]
        exps = [jnp.exp(scores[u] - row_max[u]) for u in every]
        factor = [jnp.exp(stats[u][0] - row_max[u]) for u in every]
        inverse = [
            1.0 / (jnp.sum(exps[u], axis=1, keepdims=True) + factor[u] * stats[u][1])
            for u in every
        ]
        delta = [
            inverse[u]
            * (
                jnp.sum(exps[u] * dprobs[u], axis=1, keepdims=True)
                + factor[u] * stats[u][1] * stats[u][2]
            )
            for u in every
        ]
        dscores = [(exps[u] * (dprobs[u] - delta[u])).astype(jnp.bfloat16) for u in every]
        for u, (part, head) in enumerate(units):
            back = dot(dscores[u], keys[u], ((1,), (0,))) + factor[u] * (
                slope_scr[i, rows[u], feats[u]].astype(jnp.float32)
                + (stats[u][2] - delta[u]) * base_scr[i, rows[u], feats[u]].astype(jnp.float32)
            )
            back_refs[i][rows[u], feats[u]] = (back * (inverse[u] * SCALE)).astype(jnp.bfloat16)
        for u, (part, head) in enumerate(units):
            attended = factor[u] * sum_scr[i, rows[u], feats[u]].astype(jnp.float32) + dot(
                exps[u].astype(jnp.bfloat16), values[u], ((1,), (0,))
            )
            attended = (attended * inverse[u]).astype(jnp.bfloat16)
            if shifts == (0,):
                whole_ref[pl.ds(pl.multiple_of(group * PAIR + part * BLK, BLK), BLK), feats[u]] = (
                    attended
                )
            else:
                other_refs[i][rows[u], feats[u]] = attended


def attend_memory(shifts, scalars, queries, received, grad_out, prepared, done):
    in_smem, in_vmem = (pl.BlockSpec(memory_space=space) for space in (pltpu.SMEM, pltpu.VMEM))
    count, tiles = len(shifts), len(shifts) * (PAIR // BLK)
    part = jax.ShapeDtypeStruct((PAIR, WIDTH), jnp.bfloat16)
    whole = [jax.ShapeDtypeStruct((CTX, WIDTH), jnp.bfloat16)]
    operands = [queries, grad_out, *prepared, received, *done]
    out_shape = (whole if done else [part] * count) + [part] * count
    keys_count = tiles * TOPK * BLK
    outs = pl.pallas_call(
        functools.partial(attend_memory_kernel, shifts),
        in_specs=[in_smem]
        + [pl.BlockSpec(memory_space=pl.ANY)] * 7
        + [in_vmem] * len(done),
        out_specs=[in_vmem] * len(out_shape),
        out_shape=out_shape,
        scratch_shapes=[pltpu.VMEM((count, PAIR, WIDTH), jnp.bfloat16)] * 5
        + [
            pltpu.VMEM((count, PAIR, BLK), jnp.float32),
            pltpu.VMEM((tiles, TOPK, 2, BLK, WIDTH), jnp.bfloat16),
            pltpu.SemaphoreType.DMA((tiles, TOPK)),
            pltpu.SemaphoreType.DMA((count, 6)),
        ],
        compiler_params=pltpu.CompilerParams(vmem_limit_bytes=58 * MIB),
        cost_estimate=pl.CostEstimate(
            flops=8 * BLK * keys_count * WIDTH,
            bytes_accessed=2 * 12 * CTX * WIDTH,
            transcendentals=BLK * keys_count * HEADS,
        ),
        name="attend_memory",
    )(scalars, *operands)
    return outs[:-count], outs[-count:]


PLACES = (
    (0, 0, ZN),
    (1, 0, ZN),
    (2, 0, ZN),
    (3, 0, ZN),
    *[(shift, ZN + part * HALF, HALF) for shift in range(YN) for part in range(2)],
)


def back_kernel(pos_ref, *refs):
    grad_refs, piece_refs = refs[:YN], refs[YN : YN + len(PLACES)]
    own_ref, send_ref, held, total_scr, sems = refs[YN + len(PLACES) :]
    copies = [
        pltpu.make_async_copy(piece, held.at[shift, pl.ds(first, count)], sems.at[i])
        for i, (piece, (shift, first, count)) in enumerate(zip(piece_refs, PLACES))
    ]
    stages = [copies[:YN], copies[YN::2], copies[YN + 1 :: 2]]
    for copy in stages[0] + stages[1]:
        copy.start()
    core = pos_ref[3]
    own_rows = pl.ds(pl.multiple_of(core * BLK, BLK), BLK)
    send_rows = pl.ds(pl.multiple_of((1 - core) * BLK, BLK), BLK)
    for x_shift in range(XN):
        x_index = lax.rem(pos_ref[1] + XN - x_shift, XN)
        for copy in stages[x_shift] if x_shift < len(stages) else []:
            copy.wait()
        for copy in stages[2] if x_shift == 0 else []:
            copy.start()
        blocks = slice(x_shift * ZN, (x_shift + 1) * ZN)
        total = jnp.zeros((PAIR, ZN * BLK), jnp.float32)
        for shift in range(YN):
            weight = held[shift, blocks].reshape(ZN * BLK, WIDTH)
            total += dot(grad_refs[shift][...], weight, ((1,), (1,)))
        total_scr[...] = total
        for out_ref, rows in ((send_ref, send_rows), (own_ref, own_rows)):
            for i, shift in enumerate(Z_ORDER):
                columns = pl.ds(column_of(pos_ref[0], x_index, shift), BLK)
                part = total_scr[rows, i * BLK : (i + 1) * BLK]
                out_ref[:, columns] = part.astype(out_ref.dtype)


def back_project(position, grads, pieces):
    in_vmem = pl.BlockSpec(memory_space=pltpu.VMEM)
    return pl.pallas_call(
        back_kernel,
        in_specs=[pl.BlockSpec(memory_space=pltpu.SMEM)]
        + [in_vmem] * YN
        + [pl.BlockSpec(memory_space=pl.ANY)] * len(pieces),
        out_specs=[in_vmem] * 2,
        out_shape=[
            jax.ShapeDtypeStruct((BLK, DM), jnp.float32),
            jax.ShapeDtypeStruct((BLK, DM), jnp.bfloat16),
        ],
        scratch_shapes=[
            pltpu.VMEM((YN, XN * ZN, BLK, WIDTH), jnp.bfloat16),
            pltpu.VMEM((PAIR, ZN * BLK), jnp.float32),
            pltpu.SemaphoreType.DMA((len(pieces),)),
        ],
        compiler_params=pltpu.CompilerParams(vmem_limit_bytes=20 * MIB),
        cost_estimate=pl.CostEstimate(
            flops=2 * PAIR * DM * YN * WIDTH,
            bytes_accessed=2 * (2 * PAIR * DM + DM * YN * WIDTH),
            transcendentals=0,
        ),
        name="back_project",
    )(position, *grads, *pieces)


def move(array, axis, count, shift):
    if shift % count == 0:
        return array
    return lax.ppermute(array, axis, [(i, (i + shift) % count) for i in range(count)])


def local(layer_input, w_query, local_kv, memory_kv, memory_ids, grad_out):
    position = jnp.stack([lax.axis_index(axis) for axis in ("z", "x", "y", "c")]).astype(jnp.int32)
    owner_of = memory_ids // MB_DEV
    scalars = jnp.concatenate([position, owner_of.reshape(TILES * TOPK)])
    owners = jnp.arange(OWNERS, dtype=jnp.int32)
    wanted = jnp.max(
        jnp.where(owner_of[:, :, None] == owners, (memory_ids % MB_DEV)[:, :, None], 0),
        axis=(0, 1),
    )
    weights = [move(w_query, "z", ZN, shift) for shift in Z_ORDER]
    asked = lax.all_to_all(wanted.reshape(OWNERS, 1), MEM, 0, 0, tiled=True)
    asked, weights = lax.optimization_barrier((asked, weights))
    received = lax.all_to_all(pick_blocks(asked[:, 0], memory_kv), MEM, 0, 0, tiled=True)
    own = jnp.stack(weights)
    rows = lax.all_gather(layer_input, ("y", "c"), axis=0, tiled=True)
    others = [move(own, "x", XN, shift) for shift in range(1, XN)]
    first = jnp.concatenate([others[0], others[1][: ZN // 2]])
    last = jnp.concatenate([others[1][ZN // 2 :], others[2]])
    near_parts = [own, *[move(own, "y", YN, shift) for shift in range(1, YN)]]
    first, last, near_parts = lax.optimization_barrier((first, last, near_parts))
    below, above = move(first, "y", YN, 1), move(last, "y", YN, -1)
    below_last, above_first = move(last, "y", YN, 1), move(first, "y", YN, -1)
    queries = project(scalars, rows, own, first, last)
    *sums, stats = attend_local(queries, local_kv, grad_out)
    below, above, stats = lax.optimization_barrier((below, above, stats))
    prepared = [*sums, stats]
    far_first, far_last = move(below, "y", YN, 1), move(above, "y", YN, -1)
    rest = [first, last, below, below_last, far_first, far_last, above_first, above]
    pieces = [*near_parts, *rest]
    done, far = attend_memory(FAR, scalars, queries, received, grad_out, prepared, [])
    far = {shift: move(part, "y", YN, shift) for shift, part in zip(FAR, far)}
    (attended,), (near,) = attend_memory(
        (0,), scalars, queries, received, grad_out, prepared, done
    )
    grads = [near, far[1], far[2], far[3]]
    own_part, send = back_project(scalars, grads, pieces)
    other = move(send, "c", CN, 1)
    return (attended, (own_part + other.astype(jnp.float32)).astype(jnp.bfloat16))


def solution(mesh):
    torus = Mesh(mesh.devices.reshape(ZN, XN, YN, CN), ("z", "x", "y", "c"))
    in_specs = (
        P(("z", "x", "y", "c"), None),
        P(MEM, ("y", "c")),
        P(None, MEM, ("y", "c")),
        P(MEM, None, None, ("y", "c")),
        P(MEM, None),
        P(MEM, ("y", "c")),
    )
    out_specs = (P(MEM, ("y", "c")), P(("z", "x", "y", "c"), None))
    return jax.shard_map(local, mesh=torus, in_specs=in_specs, out_specs=out_specs, check_vma=False)
```
